32 devices in a mesh: gx: 8 (over z, x), gy: 4 (over y, core).
Axes of the slice: x: 2, y: 2, z: 4, core: 2. Of those that a mesh axis runs over, the one named last changes fastest.
Arguments:
- body_force: float32 [3, 128, 128, 128], P(None, 'gx', 'gy'), may hold values from -30 to 30, as said below
- fixed_dofs: int32 [3, 128, 128, 128], P(None, 'gx', 'gy'), may hold values 0 or 1
- load_nodes: int32 [512, 3], replicated, may hold values from 0 to 127, as said below
- load_forces: float32 [3, 512], replicated, may hold values from -32 to 32
- frequencies: float32 [3, 64], replicated, may hold values from -24 to 24
- hidden_weights: float32 [3, 128, 128], replicated, may hold values from -0.5 to 0.5
- hidden_biases: float32 [3, 128], replicated, may hold values from -6 to 6
- output_weights: float32 [128], replicated, may hold values from -3 to 3
- output_bias: float32 [1], replicated, may hold values from -3 to 3
Outputs:
- displacement: float32 [3, 128, 128, 128], P(None, 'gx', 'gy')
- density: float32 [128, 128, 128], P('gx', 'gy')
The draws below stay inside these ranges and needn't reach their ends.
Inputs may be any that keep to these rules, and one draw needn't show every extreme that they name: `load_nodes`: row p gives the x, y and z index of point load p's node: column 0 below 128, column 1 below 128, column 2 below 128; several loads may share a node. `body_force`: finite values of order one to ten.
All inputs are finite; a program needn't handle non-finite values. No bound on the sum of `fixed_dofs` on one device may be relied on, other than what follows from the above.
Results may differ from the reference program's by a relative error of at most 0.00013.
Values sent between devices are 32-bit elements; how exact they have to be, the bound alone decides.
A program may use at most 128 MiB of HBM per device.

```python
import math
import jax
import jax.numpy as jnp
import numpy as np
from jax import lax

CF = 4
WIDTH = 128
FREQS = 64
LAYERS = 3
ITERS = 2
NLOAD = 512
NX = 128
NY = 128
NZ = 128


def period_sign(count):
    index = jnp.arange(count, dtype=jnp.int32)
    return (1 - 2 * (index // 2 % 2)).astype(jnp.float32)


def draw_body_force(key, part):
    grid_shape = (3, NX, NY, NZ)
    along_x = (jnp.arange(NX, dtype=jnp.float32) / NX)[None, :, None, None]
    along_y = (jnp.arange(NY, dtype=jnp.float32) / NY)[None, None, :, None]
    along_z = (jnp.arange(NZ, dtype=jnp.float32) / NZ)[None, None, None, :]
    ramp = 10.0 ** (along_x - 0.5)
    pattern = period_sign(NX)[None, :, None, None] * period_sign(NY)[None, None, :, None] * period_sign(NZ)[None, None, None, :]
    rough = jax.random.truncated_normal(key, -4.0, 4.0, grid_shape, jnp.float32)
    smooth = 1.5 * (1.0 + 0.3 * jnp.sin(2.0 * along_x + 3.0 * along_y + 1.5 * along_z))
    return (ramp * pattern * (rough + smooth)).astype(jnp.float32)


def draw_load_nodes(key, part):
    keys = jax.random.split(jax.random.fold_in(key, 7), 3)
    index_x = jax.random.randint(keys[0], (NLOAD,), 0, NX, dtype=jnp.int32)
    index_y = jax.random.randint(keys[1], (NLOAD,), 0, NY, dtype=jnp.int32)
    index_z = jax.random.randint(keys[2], (NLOAD,), 0, NZ, dtype=jnp.int32)
    index_y = index_y.at[0].set(NY - 1)
    index_x = index_x.at[1].set(0)
    index_x = index_x.at[2].set(NX - 1)
    index_z = index_z.at[3].set(NZ - 1)
    return jnp.stack([index_x, index_y, index_z], axis=1).astype(jnp.int32)


def place_ends(values, rng, smallest, high):
    dims = values.shape
    place = [jax.random.randint(jax.random.fold_in(rng, axis), (), 0, dims[axis]) for axis in range(len(dims))]
    values = values.at[tuple(place)].set(smallest)
    longest = dims.index(max(dims))
    place[longest] = (place[longest] + 1) % dims[longest]
    return values.at[tuple(place)].set(high)


def normal_values(key, extent, width, limit, kind=jnp.bfloat16):
    drawn = jax.random.normal(key, extent, jnp.float32) * width
    return jnp.minimum(jnp.maximum(drawn, -limit), limit).astype(kind)


def setup_inputs(seed: int = 0) -> dict:
    arg_keys = jax.random.split(jax.random.key(seed), 10)
    return {
        "body_force": draw_body_force(jax.random.fold_in(arg_keys[9], 71), 0),
        "fixed_dofs": place_ends((jax.random.randint(arg_keys[1], (3, NX, NY, NZ), 0, 16) < 1).astype(jnp.int32), jax.random.fold_in(arg_keys[1], 1), 0, 1),
        "load_nodes": draw_load_nodes(jax.random.fold_in(arg_keys[9], 71), 0),
        "load_forces": normal_values(arg_keys[3], (3, NLOAD), 5.0, 32.0, jnp.float32),
        "frequencies": normal_values(arg_keys[4], (3, FREQS), 4.0, 24.0, jnp.float32),
        "hidden_weights": normal_values(arg_keys[5], (LAYERS, WIDTH, WIDTH), WIDTH ** -0.5, 0.5, jnp.float32),
        "hidden_biases": normal_values(arg_keys[6], (LAYERS, WIDTH), 0.5, 6.0, jnp.float32),
        "output_weights": normal_values(arg_keys[7], (WIDTH,), 0.2, 3.0, jnp.float32),
        "output_bias": normal_values(arg_keys[8], (1,), 1.0, 3.0, jnp.float32),
    }


full_turn = 2.0 * math.pi
highest = lax.Precision.HIGHEST

def element_stiffness():
    poisson = 0.3
    lame_first = poisson / ((1.0 + poisson) * (1.0 - 2.0 * poisson))
    lame_second = 1.0 / (2.0 * (1.0 + poisson))
    elastic = np.zeros((6, 6))
    elastic[:3, :3] = lame_first
    elastic[np.arange(3), np.arange(3)] += 2.0 * lame_second
    elastic[np.arange(3, 6), np.arange(3, 6)] = lame_second
    gauss = 1.0 / math.sqrt(3.0)
    stiffness = np.zeros((24, 24))
    for point in range(8):
        where_at = [gauss * (2 * (point >> which & 1) - 1) for which in range(3)]
        strain = np.zeros((6, 24))
        for corner in range(8):
            signs = [2 * (corner >> which & 1) - 1 for which in range(3)]
            slopes = []
            for which in range(3):
                value = 0.25 * signs[which]
                for other in range(3):
                    if other != which:
                        value = value * (1.0 + signs[other] * where_at[other])
                slopes.append(value)
            column = 3 * corner
            strain[0, column] = slopes[0]
            strain[1, column + 1] = slopes[1]
            strain[2, column + 2] = slopes[2]
            strain[3, column] = slopes[1]
            strain[3, column + 1] = slopes[0]
            strain[4, column + 1] = slopes[2]
            strain[4, column + 2] = slopes[1]
            strain[5, column] = slopes[2]
            strain[5, column + 2] = slopes[0]
        stiffness = stiffness + strain.T @ elastic @ strain * 0.125
    return jnp.asarray(stiffness, dtype=jnp.float32)

def corner_offsets(corner):
    return (corner & 1, corner >> 1 & 1, corner >> 2 & 1)

def z_shift(values, offset):
    widths = [(0, 0)] * (values.ndim - 1)
    if offset > 0:
        return jnp.pad(values[..., 1:], widths + [(0, 1)])
    return jnp.pad(values[..., :-1], widths + [(1, 0)])

def coarse_density(begin_x, begin_y, count_x, count_y, count_z, total_x, total_y, total_z, frequencies, hidden_weights, hidden_biases, output_weights, output_bias):
    along_x = ((begin_x + jnp.arange(count_x, dtype=jnp.int32)).astype(jnp.float32) + 0.5) / float(total_x)
    along_y = ((begin_y + jnp.arange(count_y, dtype=jnp.int32)).astype(jnp.float32) + 0.5) / float(total_y)
    along_z = (jnp.arange(count_z, dtype=jnp.int32).astype(jnp.float32) + 0.5) / float(total_z)
    grid_shape = (count_x, count_y, count_z)
    centres = jnp.stack([jnp.broadcast_to(along_x[:, None, None], grid_shape).reshape(-1), jnp.broadcast_to(along_y[None, :, None], grid_shape).reshape(-1), jnp.broadcast_to(along_z[None, None, :], grid_shape).reshape(-1)], axis=0)
    phases = jnp.dot(frequencies.T, centres, precision=highest, preferred_element_type=jnp.float32) * full_turn
    hidden = jnp.concatenate([jnp.sin(phases), jnp.cos(phases)], axis=0)
    for layer in range(hidden_weights.shape[0]):
        mixed = jnp.dot(hidden_weights[layer].T, hidden, precision=highest, preferred_element_type=jnp.float32)
        hidden = jax.nn.silu(mixed + hidden_biases[layer][:, None])
    logits = jnp.dot(output_weights, hidden, precision=highest, preferred_element_type=jnp.float32) + output_bias[0]
    return jax.nn.sigmoid(logits).reshape(grid_shape)

def upsample(coarse):
    across, along, height = coarse.shape
    spread = jnp.broadcast_to(coarse[:, None, :, None, :, None], (across, CF, along, CF, height, CF))
    return spread.reshape(across * CF, along * CF, height * CF)

def cone_filter(padded, count_x, count_y):
    result = jnp.zeros((count_x, count_y, padded.shape[2]), jnp.float32)
    for shift_x in (-1, 0, 1):
        for shift_y in (-1, 0, 1):
            for shift_z in (-1, 0, 1):
                weight = 2.0 - math.sqrt(shift_x * shift_x + shift_y * shift_y + shift_z * shift_z)
                piece = padded[1 + shift_x:1 + shift_x + count_x, 1 + shift_y:1 + shift_y + count_y]
                if shift_z != 0:
                    piece = z_shift(piece, shift_z)
                result = result + weight * piece
    return result

def corner_products(nodes, young, stiffness):
    across, along, height = young.shape
    pieces = []
    for corner in range(8):
        off_x, off_y, off_z = corner_offsets(corner)
        piece = nodes[:, off_x:off_x + across, off_y:off_y + along]
        if off_z:
            piece = z_shift(piece, 1)
        pieces.append(piece)
    stacked = jnp.concatenate(pieces, axis=0).reshape(24, across * along * height)
    products = jnp.dot(stiffness, stacked, precision=highest, preferred_element_type=jnp.float32)
    return products.reshape(24, across, along, height) * young[None]

def interior_forces(products):
    across, along = (products.shape[1], products.shape[2])
    result = jnp.zeros((3, across - 1, along - 1, products.shape[3]), jnp.float32)
    for corner in range(8):
        off_x, off_y, off_z = corner_offsets(corner)
        piece = products[3 * corner:3 * corner + 3, 1 - off_x:across - off_x, 1 - off_y:along - off_y]
        if off_z:
            piece = z_shift(piece, -1)
        result = result + piece
    return result

def recompute_forces(nodes_ext, young_ext, stiffness):
    planes = nodes_ext.shape[1] - 2
    count = planes // CF

    def block(index):
        begin = index * CF
        nodes_block = lax.dynamic_slice_in_dim(nodes_ext, begin, CF + 2, 1)
        young_block = lax.dynamic_slice_in_dim(young_ext, begin, CF + 1, 0)
        return interior_forces(corner_products(nodes_block, young_block, stiffness))
    blocks = lax.map(block, jnp.arange(count, dtype=jnp.int32))
    return jnp.moveaxis(blocks, 0, 1).reshape(3, planes, nodes_ext.shape[2] - 2, nodes_ext.shape[3])

def stiffness_diagonal(young_ext, stiffness):
    across, along = (young_ext.shape[0] - 1, young_ext.shape[1] - 1)
    entries = jnp.diagonal(stiffness)
    result = jnp.zeros((3, across, along, young_ext.shape[2]), jnp.float32)
    for corner in range(8):
        off_x, off_y, off_z = corner_offsets(corner)
        piece = young_ext[1 - off_x:1 - off_x + across, 1 - off_y:1 - off_y + along]
        if off_z:
            piece = z_shift(piece, -1)
        result = result + entries[3 * corner:3 * corner + 3][:, None, None, None] * piece[None]
    return result

def reference(body_force, fixed_dofs, load_nodes, load_forces, frequencies, hidden_weights, hidden_biases, output_weights, output_bias):
    stiffness = element_stiffness()
    coarse = coarse_density(0, 0, NX // CF, NY // CF, NZ // CF, NX // CF, NY // CF, NZ // CF, frequencies, hidden_weights, hidden_biases, output_weights, output_bias)
    raw = upsample(coarse)
    rim_widths = ((1, 1), (1, 1), (0, 0))
    inside = jnp.pad(jnp.ones((NX, NY, NZ), jnp.float32), rim_widths)
    density = cone_filter(jnp.pad(raw, rim_widths), NX, NY) / cone_filter(inside, NX, NY)
    young = 0.02 + 0.98 * density ** 3
    young_ext = jnp.pad(young, ((1, 0), (1, 0), (0, 0)))
    free_dofs = 1.0 - fixed_dofs.astype(jnp.float32)
    jacobi = free_dofs * stiffness_diagonal(young_ext, stiffness) + (1.0 - free_dofs)
    loaded = body_force.at[:, load_nodes[:, 0], load_nodes[:, 1], load_nodes[:, 2]].add(load_forces)
    rhs = free_dofs * loaded

    def apply_operator(field):
        padded = jnp.pad(field, ((0, 0), (1, 1), (1, 1), (0, 0)))
        return free_dofs * recompute_forces(padded, young_ext, stiffness)
    displacement = jnp.zeros_like(rhs)
    residual = rhs
    scaled = residual / jacobi
    direction = scaled
    norm_now = jnp.sum(residual * scaled)
    for iteration in range(ITERS):
        image = apply_operator(direction)
        alpha = norm_now / jnp.sum(direction * image)
        displacement = displacement + alpha * direction
        residual = residual - alpha * image
        if iteration + 1 < ITERS:
            scaled = residual / jacobi
            norm_next = jnp.sum(residual * scaled)
            direction = scaled + norm_next / norm_now * direction
            norm_now = norm_next
    return (displacement, density)
```

```python
import functools
import math

import jax
import jax.numpy as jnp
from jax import lax
from jax.experimental import pallas as pl
from jax.experimental.pallas import tpu as pltpu
from jax.sharding import PartitionSpec as P

MESH = pl.DeviceIdType.MESH
CF = 4
HALO = 2
f32 = jnp.float32
bf16 = jnp.bfloat16
POISSON = 0.3
LAM = POISSON / ((1.0 + POISSON) * (1.0 - 2.0 * POISSON))
MU = 1.0 / (2.0 * (1.0 + POISSON))
TWO_PI = 2.0 * math.pi
DIAG = ((LAM + 4.0 * MU) * (1.0 + 2.0 / 3.0 + 1.0 / 9.0)) / 16.0
FULL = pl.BlockSpec(memory_space=pltpu.VMEM)


def halo_kernel(bf, fx, xb, xf, yh, ch, ys, send, recv):
    gx, gy = lax.axis_index("gx"), lax.axis_index("gy")
    nx, ny = lax.axis_size("gx"), lax.axis_size("gy")
    planes, rows = bf.shape[1], bf.shape[2]

    def at(dx, dy):
        return (lax.rem(gx + dx + nx, nx), lax.rem(gy + dy + ny, ny))

    barrier = pltpu.get_barrier_semaphore()
    around = [(dx, dy) for dx in (-1, 0, 1) for dy in (-1, 0, 1) if dx or dy]
    for dx, dy in around:
        pl.semaphore_signal(barrier, inc=1, device_id=at(dx, dy), device_id_type=MESH)
    for side in range(2):
        first = 0 if side == 0 else rows - HALO
        for c in range(3):
            span = slice(HALO * c, HALO * c + HALO)
            ys[side, :, 0, span, :] = bf[c, :, first : first + HALO, :]
            ys[side, :, 1, span, :] = 1.0 - fx[c, :, first : first + HALO, :].astype(f32)
        ys[side, :, :, 3 * HALO :, :] = jnp.zeros((planes, 2, 8 - 3 * HALO, bf.shape[3]), f32)
    pl.semaphore_wait(barrier, len(around))
    copies = []

    def launch(src, dst, where):
        index = len(copies)
        copy = pltpu.make_async_remote_copy(
            src_ref=src,
            dst_ref=dst,
            send_sem=send.at[index],
            recv_sem=recv.at[index],
            device_id=where,
            device_id_type=MESH,
        )
        copy.start()
        copies.append(copy)

    for side in range(2):
        step = 2 * side - 1
        near = pl.ds(0 if side == 0 else planes - HALO, HALO)
        launch(bf.at[:, near], xb.at[1 - side], at(step, 0))
        launch(fx.at[:, near], xf.at[1 - side], at(step, 0))
        launch(ys.at[side], yh.at[1 - side], at(0, step))
        for other in range(2):
            launch(
                ys.at[other, near], ch.at[1 - side, 1 - other], at(step, 2 * other - 1)
            )
    for copy in copies:
        copy.wait()


def sum_kernel(mine, total, along, across, part, send, recv):
    gx, gy = lax.axis_index("gx"), lax.axis_index("gy")
    nx, ny = lax.axis_size("gx"), lax.axis_size("gy")
    barrier = pltpu.get_barrier_semaphore()
    for k in range(1, nx):
        pl.semaphore_signal(
            barrier, inc=1, device_id=(lax.rem(gx + k, nx), gy), device_id_type=MESH
        )
    for k in range(1, ny):
        pl.semaphore_signal(
            barrier, inc=1, device_id=(gx, lax.rem(gy + k, ny)), device_id_type=MESH
        )
    pl.semaphore_wait(barrier, nx + ny - 2)

    def exchange(src, dst, count, base, where):
        copies = []
        for k in range(1, count):
            copy = pltpu.make_async_remote_copy(
                src_ref=src,
                dst_ref=dst.at[k - 1],
                send_sem=send.at[base + k - 1],
                recv_sem=recv.at[base + k - 1],
                device_id=where(k),
                device_id_type=MESH,
            )
            copy.start()
            copies.append(copy)
        for copy in copies:
            copy.wait()

    exchange(mine, along, nx, 0, lambda k: (lax.rem(gx + k, nx), gy))
    part[...] = mine[...] + jnp.sum(along[...], axis=0)
    exchange(part, across, ny, nx - 1, lambda k: (gx, lax.rem(gy + k, ny)))
    total[...] = part[...] + jnp.sum(across[...], axis=0)


def split(value):
    high = value.astype(bf16)
    return high, (value - high.astype(f32)).astype(bf16)


def work_kernel(
    bf, fx, xb, xf, yh, ch, nodes, loads, freq, hw, hb, ow, ob,
    z_out, q_out, dens, sums,
    wide, up, filt, ye, inv_s, force, free_s, z_s, q_s,
):
    gx, gy = lax.axis_index("gx"), lax.axis_index("gy")
    nx, ny = lax.axis_size("gx"), lax.axis_size("gy")
    planes, rows, height = bf.shape[1], bf.shape[2], bf.shape[3]
    cx, cy, cz = planes // CF + 2, rows // CF + 2, height // CF
    tall = cy * CF
    deep = planes + 2 * HALO
    total_cx, total_cy = nx * (planes // CF), ny * (rows // CF)
    plane = (tall, height)
    lane = lax.broadcasted_iota(jnp.int32, plane, 1)
    row = lax.broadcasted_iota(jnp.int32, plane, 0)
    own_row = ((row >= CF) & (row < CF + rows)).astype(f32)
    cell_row = gy * rows - CF + row
    inside_y = ((cell_row >= 0) & (cell_row < ny * rows)).astype(f32)

    def up_z(v):
        return jnp.where(lane < height - 1, pltpu.roll(v, height - 1, 1), 0.0)

    def down_z(v):
        return jnp.where(lane > 0, pltpu.roll(v, 1, 1), 0.0)

    def up_y(v):
        return pltpu.roll(v, tall - 1, 0)

    def down_y(v):
        return pltpu.roll(v, 1, 0)

    def fold(v):
        return jnp.sum(v.reshape(tall // 8, 8, height), axis=0)

    layers, width = hw.shape[0], hw.shape[2]
    for layer in range(layers):
        high, low = split(hw[layer])
        both = jnp.concatenate([high, low], axis=1)
        wide[layer] = jnp.concatenate([both, both], axis=0)
    high, low = split(jnp.broadcast_to(ow[...], (height, width)))
    wide_out = jnp.concatenate(
        [jnp.concatenate([high, high], axis=1), jnp.concatenate([low, low], axis=1)], axis=0
    )
    turn = jnp.concatenate([freq[...], freq[...]], axis=1)
    half = freq.shape[1]

    def index_rows(count):
        return lax.broadcasted_iota(jnp.int32, (count, 2 * half), 0)

    def wave(t):
        t = (t - jnp.floor(t + 0.5)) * TWO_PI
        return jnp.sin(t), jnp.cos(t)

    quarter = (lax.broadcasted_iota(jnp.int32, (1, 2 * half), 1) >= half).astype(f32) * 0.25
    at_z = (index_rows(cz).astype(f32) + 0.5) / float(cz)
    sin_v, cos_v = wave(at_z * turn[2:3])
    padded_cy = -(-cy // 8) * 8
    at_y = ((gy * (rows // CF) - 1 + index_rows(padded_cy)).astype(f32) + 0.5) / float(total_cy)
    turn_y = at_y * turn[1:2]
    pick = (
        lax.broadcasted_iota(jnp.int32, (cz, height), 1) // CF
        == lax.broadcasted_iota(jnp.int32, (cz, height), 0)
    ).astype(f32)
    bias_out = ob[0, 0]

    def cells(ix, _):
        index_x = gx * (planes // CF) - 1 + ix
        inside_x = jnp.where((index_x >= 0) & (index_x < total_cx), 1.0, 0.0).astype(f32)
        at_x = (index_x.astype(f32) + 0.5) / float(total_cx)
        sin_u, cos_u = wave(turn_y + (at_x * turn[0:1] + quarter))
        hidden = jnp.concatenate(
            [sin_u[j : j + 1] * cos_v + cos_u[j : j + 1] * sin_v for j in range(cy)], axis=0
        )
        for layer in range(layers):
            lhs = jnp.concatenate(split(hidden), axis=1)
            out = jnp.dot(lhs, wide[layer], preferred_element_type=f32)
            mixed = out[:, :width] + out[:, width:] + hb[layer : layer + 1, :]
            hidden = mixed / (1.0 + jnp.exp(jnp.minimum(-mixed, 80.0)))
        lhs = jnp.concatenate(split(hidden), axis=1)
        out = lax.dot_general(
            lhs, wide_out, (((1,), (1,)), ((), ())), preferred_element_type=f32
        )
        spread = (out[:, :height] + out[:, height:]).reshape(cy, cz, height)
        logits = jnp.sum(spread * pick[None], axis=1) + bias_out
        coarse = 1.0 / (1.0 + jnp.exp(jnp.minimum(-logits, 80.0)))
        for j in range(cy):
            up[ix, CF * j : CF * j + CF, :] = jnp.broadcast_to(coarse[j : j + 1], (CF, height))
        inside = inside_y * inside_x
        for base, values in ((0, up[ix] * inside), (2, inside)):
            beside = up_z(values) + down_z(values)
            w2, w3 = 2.0 - math.sqrt(2.0), 2.0 - math.sqrt(3.0)
            one = values + w2 * beside
            two = w2 * values + w3 * beside
            filt[base, ix] = 2.0 * values + beside + up_y(one) + down_y(one)
            filt[base + 1, ix] = one + up_y(two) + down_y(two)
        return 0

    lax.fori_loop(0, cx, cells, 0)

    def filtered(i, _):
        here, back, ahead = (i + 1) // CF, i // CF, (i + 2) // CF
        top = filt[0, here] + filt[1, back] + filt[1, ahead]
        bottom = filt[2, here] + filt[3, back] + filt[3, ahead]
        value = top / jnp.maximum(bottom, 0.5)
        index_x = gx * (planes // CF) - 1 + here
        inside_x = jnp.where((index_x >= 0) & (index_x < total_cx), 1.0, 0.0).astype(f32)
        ye[i] = (0.02 + 0.98 * value * value * value) * (inside_y * inside_x)

        @pl.when((i >= HALO + 1) & (i < HALO + 1 + planes))
        def _():
            dens[i - HALO - 1] = value[CF : CF + rows]

        return 0

    lax.fori_loop(0, deep + 1, filtered, 0)

    count = nodes.shape[0]
    eye = (
        lax.broadcasted_iota(jnp.int32, (8, 3), 0) == lax.broadcasted_iota(jnp.int32, (8, 3), 1)
    ).astype(f32)
    flat = lax.dot_general(
        eye,
        nodes[...].astype(f32),
        (((1,), (1,)), ((), ())),
        precision=lax.Precision.HIGHEST,
        preferred_element_type=f32,
    )
    flat = (flat + 0.5).astype(jnp.int32)
    local_x = flat[0:1] - gx * planes + HALO
    local_y = flat[1:2] - gy * rows + CF
    near = (local_x >= 0) & (local_x < deep) & (local_y >= 0) & (local_y < tall)
    place = jnp.where(near, local_x * tall + local_y, -1)
    hit_z = lax.broadcasted_iota(jnp.int32, (height, count), 0) == flat[2:3]
    pieces = [[], [], []]
    for c in range(3):
        rest = loads[c : c + 1, :]
        for term in range(3):
            high = rest.astype(bf16).astype(f32)
            pieces[term].append(jnp.where(hit_z, high, 0.0).astype(bf16))
            rest = rest - high
    table = jnp.concatenate(pieces[0] + pieces[1] + pieces[2], axis=0)
    group = 4

    def place_loads(g, _):
        here = g * (group * tall) + lax.broadcasted_iota(jnp.int32, (group * tall, count), 0)
        hit = jnp.where(here == place, 1.0, 0.0).astype(bf16)
        out = lax.dot_general(hit, table, (((1,), (1,)), ((), ())), preferred_element_type=f32)
        for c in range(3):
            parts = [out[:, (3 * t + c) * height : (3 * t + c + 1) * height] for t in range(3)]
            z_s[c, pl.ds(g * group, group)] = ((parts[2] + parts[1]) + parts[0]).reshape(
                group, tall, height
            )
        return 0

    lax.fori_loop(0, deep // group, place_loads, 0)

    edge = CF - HALO
    for ref in (force, free_s):
        ref[:, :, :edge, :] = jnp.zeros((3, deep, edge, height), f32)
        ref[:, :, tall - edge :, :] = jnp.zeros((3, deep, edge, height), f32)
    own = slice(CF, CF + rows)
    force[:, HALO : HALO + planes, own] = bf[...]
    free_s[:, HALO : HALO + planes, own] = 1.0 - fx[...].astype(f32)
    for side in range(2):
        first = 0 if side == 0 else deep - HALO
        force[:, first : first + HALO, own] = xb[side]
        free_s[:, first : first + HALO, own] = 1.0 - xf[side].astype(f32)
        start = edge if side == 0 else CF + rows
        for c in range(3):
            span = slice(HALO * c, HALO * c + HALO)
            for ref, which in ((force, 0), (free_s, 1)):
                ref[c, HALO : HALO + planes, start : start + HALO] = yh[side, :, which, span]
                for other in range(2):
                    begin = 0 if other == 0 else deep - HALO
                    ref[c, begin : begin + HALO, start : start + HALO] = ch[
                        other, side, :, which, span
                    ]
    node_row = gy * rows - CF + row
    in_y = ((node_row >= 0) & (node_row < ny * rows)).astype(f32)

    def own_plane(m):
        return jnp.where((m >= HALO) & (m < HALO + planes), 1.0, 0.0).astype(f32)

    def begin(m, total):
        node_x = gx * planes - HALO + m
        in_x = jnp.where((node_x >= 0) & (node_x < nx * planes), 1.0, 0.0).astype(f32)
        s = ye[m] + ye[m + 1]
        s = s + down_y(s)
        s = s + down_z(s)
        inv = 1.0 / jnp.maximum(DIAG * s, 1e-4)
        inv_s[m] = inv
        counted = own_row * own_plane(m)
        inside = in_y * in_x
        part = jnp.zeros(plane, f32)
        for c in range(3):
            free = free_s[c, m] * inside
            free_s[c, m] = free
            rhs = free * (force[c, m] + z_s[c, m])
            z0 = rhs * inv
            z_s[c, m] = z0
            part = part + rhs * z0
        return total + fold(part * counted)

    zero = jnp.zeros((8, height), f32)
    sum_a = lax.fori_loop(0, deep, begin, zero)

    def element_forces(src, e):
        modes = []
        for c in range(3):
            low, high = src[c, e], src[c, e + 1]
            by = {}
            for name_x, v in (("S", low + high), ("D", high - low)):
                w = up_y(v)
                for name_y, t in (("S", v + w), ("D", w - v)):
                    u = up_z(t)
                    if name_x + name_y != "SS":
                        by[name_x + name_y + "S"] = t + u
                    by[name_x + name_y + "D"] = u - t
            modes.append(by)
        x, y, z = modes
        y1 = ye[e + 1] * (1.0 / 16.0)
        y3 = y1 * (1.0 / 3.0)
        out = ({}, {}, {})
        trace = LAM * (x["DSS"] + y["SDS"] + z["SSD"])
        out[0]["DSS"] = y1 * (trace + (2 * MU) * x["DSS"])
        out[1]["SDS"] = y1 * (trace + (2 * MU) * y["SDS"])
        out[2]["SSD"] = y1 * (trace + (2 * MU) * z["SSD"])
        ym = y1 * MU
        out[0]["SDS"] = out[1]["DSS"] = ym * (x["SDS"] + y["DSS"])
        out[0]["SSD"] = out[2]["DSS"] = ym * (x["SSD"] + z["DSS"])
        out[1]["SSD"] = out[2]["SDS"] = ym * (y["SSD"] + z["SDS"])
        t = LAM * (y["DDS"] + z["DSD"])
        out[1]["DDS"] = y3 * (t + (3 * MU) * y["DDS"])
        out[2]["DSD"] = y3 * (t + (3 * MU) * z["DSD"])
        t = LAM * (x["DDS"] + z["SDD"])
        out[0]["DDS"] = y3 * (t + (3 * MU) * x["DDS"])
        out[2]["SDD"] = y3 * (t + (3 * MU) * z["SDD"])
        t = LAM * (x["DSD"] + y["SDD"])
        out[0]["DSD"] = y3 * (t + (3 * MU) * x["DSD"])
        out[1]["SDD"] = y3 * (t + (3 * MU) * y["SDD"])
        ym = y3 * MU
        p, q, r = y["DSD"], z["DDS"], x["SDD"]
        out[1]["DSD"] = ym * ((p + q) + (r + p))
        out[2]["DDS"] = ym * ((p + q) + (r + q))
        out[0]["SDD"] = ym * ((r + q) + (r + p))
        y9 = y1 * ((LAM + 4.0 * MU) / 9.0)
        for c in range(3):
            out[c]["DDD"] = y9 * modes[c]["DDD"]
        lows, highs = [], []
        for c in range(3):
            by_x = []
            for name_x in "SD":
                by_y = []
                for name_y in "SD":
                    d = out[c][name_x + name_y + "D"]
                    if name_x + name_y == "SS":
                        by_y.append(down_z(d) - d)
                    else:
                        s = out[c][name_x + name_y + "S"]
                        by_y.append((s - d) + down_z(s + d))
                s, d = by_y
                by_x.append((s - d) + down_y(s + d))
            s, d = by_x
            lows.append(s - d)
            highs.append(s + d)
        return lows, highs

    def first(e, carry):
        c0, c1, c2, sum_b, sum_c = carry
        lows, highs = element_forces(z_s, e)
        inv = inv_s[e]
        counted = own_row * own_plane(e)
        part_b = jnp.zeros(plane, f32)
        part_c = jnp.zeros(plane, f32)
        for c, before in enumerate((c0, c1, c2)):
            w = free_s[c, e] * (before + lows[c])
            q = w * inv
            q_s[c, e] = q
            part_b = part_b + w * z_s[c, e]
            part_c = part_c + w * q
        return (*highs, sum_b + fold(part_b * counted), sum_c + fold(part_c * counted))

    blank = jnp.zeros(plane, f32)
    *_, sum_b, sum_c = lax.fori_loop(0, deep - 1, first, (blank, blank, blank, zero, zero))

    def second(e, carry):
        c0, c1, c2, sum_d = carry
        lows, highs = element_forces(q_s, e)
        counted = own_row * own_plane(e)
        part = jnp.zeros(plane, f32)
        for c, before in enumerate((c0, c1, c2)):
            part = part + free_s[c, e] * (before + lows[c]) * q_s[c, e]
        return (*highs, sum_d + fold(part * counted))

    *_, sum_d = lax.fori_loop(1, HALO + planes, second, (blank, blank, blank, zero))
    z_out[...] = z_s[:, HALO : HALO + planes, own]
    q_out[...] = q_s[:, HALO : HALO + planes, own]
    sums[...] = jnp.zeros_like(sums)
    for index, value in enumerate((sum_a, sum_b, sum_c, sum_d)):
        sums[index : index + 1, :] = jnp.sum(value, axis=0, keepdims=True)


def per_device(bf, fx, nodes, loads, freq, hw, hb, ow, ob):
    nx, ny = lax.axis_size("gx"), lax.axis_size("gy")
    _, planes, rows, height = bf.shape
    shape = jax.ShapeDtypeStruct
    halo = (2, 3, HALO, rows, height)
    packed = (2, planes, 2, 8, height)
    corner = (2, 2, HALO, 2, 8, height)
    xb, xf, yh, ch = pl.pallas_call(
        halo_kernel,
        out_shape=[
            shape(halo, f32), shape(halo, jnp.int32), shape(packed, f32), shape(corner, f32)
        ],
        in_specs=[FULL] * 2,
        out_specs=[FULL] * 4,
        scratch_shapes=[
            pltpu.VMEM(packed, f32),
            pltpu.SemaphoreType.DMA((10,)),
            pltpu.SemaphoreType.DMA((10,)),
        ],
        compiler_params=pltpu.CompilerParams(
            collective_id=0, has_side_effects=True, vmem_limit_bytes=16 << 20
        ),
    )(bf, fx)
    cx, tall, deep = planes // CF + 2, rows + 2 * CF, planes + 2 * HALO
    width = hw.shape[2]
    field = pltpu.VMEM((3, deep, tall, height), f32)
    z0, q, density, sums = pl.pallas_call(
        work_kernel,
        out_shape=[
            shape(bf.shape, f32),
            shape(bf.shape, f32),
            shape(bf.shape[1:], f32),
            shape((8, height), f32),
        ],
        in_specs=[FULL] * 12 + [pl.BlockSpec(memory_space=pltpu.SMEM)],
        out_specs=[FULL] * 4,
        scratch_shapes=[
            pltpu.VMEM((hw.shape[0], 2 * width, 2 * width), bf16),
            pltpu.VMEM((cx, tall, height), f32),
            pltpu.VMEM((4, cx, tall, height), f32),
            pltpu.VMEM((deep + 1, tall, height), f32),
            pltpu.VMEM((deep, tall, height), f32),
            field,
            field,
            field,
            field,
        ],
        compiler_params=pltpu.CompilerParams(vmem_limit_bytes=40 << 20),
    )(bf, fx, xb, xf, yh, ch, nodes, loads, freq, hw, hb, ow.reshape(1, -1), ob.reshape(1, 1))
    total = pl.pallas_call(
        sum_kernel,
        out_shape=shape(sums.shape, f32),
        in_specs=[FULL],
        out_specs=FULL,
        scratch_shapes=[
            pltpu.VMEM((nx - 1, *sums.shape), f32),
            pltpu.VMEM((ny - 1, *sums.shape), f32),
            pltpu.VMEM(sums.shape, f32),
            pltpu.SemaphoreType.DMA((nx + ny - 2,)),
            pltpu.SemaphoreType.DMA((nx + ny - 2,)),
        ],
        compiler_params=pltpu.CompilerParams(
            collective_id=1, has_side_effects=True, vmem_limit_bytes=16 << 20
        ),
    )(sums)
    scalars = jnp.sum(total, axis=1)
    a, b, c, d = (scalars[i] for i in range(4))
    alpha = a / b
    next_rz = a - 2.0 * alpha * b + alpha * alpha * c
    beta = next_rz / a
    bent = b - 2.0 * alpha * c + alpha * alpha * d
    energy = bent + 2.0 * beta * (b - alpha * c) + beta * beta * b
    alpha_next = next_rz / energy
    along_z = alpha + alpha_next * (1.0 + beta)
    displacement = along_z * z0 - (alpha_next * alpha) * q
    return displacement, density


def solution(mesh):
    grid = P(None, "gx", "gy", None)
    return jax.shard_map(
        per_device,
        mesh=mesh,
        in_specs=(grid, grid, P(), P(), P(), P(), P(), P(), P()),
        out_specs=(grid, P("gx", "gy", None)),
        check_vma=False,
    )
```

```python
import functools
import math

import jax
import jax.numpy as jnp
from jax import lax
from jax.experimental import pallas as pl
from jax.experimental.pallas import tpu as pltpu
from jax.sharding import PartitionSpec as P

MESH = pl.DeviceIdType.MESH
CF = 4
HALO = 2
f32 = jnp.float32
bf16 = jnp.bfloat16
POISSON = 0.3
LAM = POISSON / ((1.0 + POISSON) * (1.0 - 2.0 * POISSON))
MU = 1.0 / (2.0 * (1.0 + POISSON))
TWO_PI = 2.0 * math.pi
DIAG = ((LAM + 4.0 * MU) * (1.0 + 2.0 / 3.0 + 1.0 / 9.0)) / 16.0
FULL = pl.BlockSpec(memory_space=pltpu.VMEM)


def split(value):
    high = value.astype(bf16)
    return high, (value - high.astype(f32)).astype(bf16)


def whole_kernel(
    bf_far, fx_far, nodes, loads, freq, hw, hb, ow, ob,
    x_out, dens,
    bf, fx, xb, xf, yh, ch, ys, along, across, mine, part,
    wide, up, filt, ye, inv_s, force, free_s, z_s, q_s,
    local, send, recv, sum_send, sum_recv,
):
    gx, gy = lax.axis_index("gx"), lax.axis_index("gy")
    nx, ny = lax.axis_size("gx"), lax.axis_size("gy")
    planes, rows, height = bf.shape[1], bf.shape[2], bf.shape[3]

    fetches = []
    for c in range(3):
        for far, near, index in ((bf_far, bf, c), (fx_far, fx, 3 + c)):
            fetch = pltpu.make_async_copy(far.at[c], near.at[c], local.at[index])
            fetch.start()
            fetches.append(fetch)
    for ref in (xb, xf, yh, ch):
        ref[...] = jnp.zeros_like(ref)

    def at(dx, dy):
        return (lax.rem(gx + dx + nx, nx), lax.rem(gy + dy + ny, ny))

    barrier = pltpu.get_barrier_semaphore()
    partners = [at(dx, dy) for dx in (-1, 1) for dy in (-1, 1)]
    partners += [at(k, 0) for k in range(1, nx)] + [at(0, k) for k in range(1, ny)]
    for partner in partners:
        pl.semaphore_signal(barrier, inc=1, device_id=partner, device_id_type=MESH)
    pl.semaphore_wait(barrier, len(partners))

    def there(dx, dy):
        ok = None
        for d, here, count in ((dx, gx, nx), (dy, gy, ny)):
            if d:
                one = here > 0 if d < 0 else here < count - 1
                ok = one if ok is None else ok & one
        return ok

    copies = []

    def launch(src, dst, step):
        index = len(copies)
        copy = pltpu.make_async_remote_copy(
            src_ref=src,
            dst_ref=dst,
            send_sem=send.at[index],
            recv_sem=recv.at[index],
            device_id=at(*step),
            device_id_type=MESH,
        )
        copies.append((copy, step))
        pl.when(there(*step))(copy.start)

    for side in range(2):
        near = pl.ds(0 if side == 0 else planes - HALO, HALO)
        launch(bf_far.at[:, near], xb.at[1 - side], (2 * side - 1, 0))
        launch(fx_far.at[:, near], xf.at[1 - side], (2 * side - 1, 0))
    for fetch in fetches:
        fetch.wait()
    for side in range(2):
        begin_row = 0 if side == 0 else rows - HALO
        for c in range(3):
            span = slice(HALO * c, HALO * c + HALO)
            ys[side, :, 0, span, :] = bf[c, :, begin_row : begin_row + HALO, :]
            ys[side, :, 1, span, :] = 1.0 - fx[c, :, begin_row : begin_row + HALO, :].astype(f32)
        ys[side, :, :, 3 * HALO :, :] = jnp.zeros((planes, 2, 8 - 3 * HALO, height), f32)
    for side in range(2):
        launch(ys.at[side], yh.at[1 - side], (0, 2 * side - 1))
        near = pl.ds(0 if side == 0 else planes - HALO, HALO)
        for other in range(2):
            launch(
                ys.at[other, near], ch.at[1 - side, 1 - other], (2 * side - 1, 2 * other - 1)
            )

    cx, cy, cz = planes // CF + 2, rows // CF + 2, height // CF
    tall = cy * CF
    deep = planes + 2 * HALO
    total_cx, total_cy = nx * (planes // CF), ny * (rows // CF)
    plane = (tall, height)
    lane = lax.broadcasted_iota(jnp.int32, plane, 1)
    row = lax.broadcasted_iota(jnp.int32, plane, 0)
    own_row = ((row >= CF) & (row < CF + rows)).astype(f32)
    cell_row = gy * rows - CF + row
    inside_y = ((cell_row >= 0) & (cell_row < ny * rows)).astype(f32)

    def up_z(v):
        return jnp.where(lane < height - 1, pltpu.roll(v, height - 1, 1), 0.0)

    def down_z(v):
        return jnp.where(lane > 0, pltpu.roll(v, 1, 1), 0.0)

    def up_y(v):
        return pltpu.roll(v, tall - 1, 0)

    def down_y(v):
        return pltpu.roll(v, 1, 0)

    def fold(v):
        return jnp.sum(v.reshape(tall // 8, 8, height), axis=0)

    layers, width = hw.shape[0], hw.shape[2]
    for layer in range(layers):
        high, low = split(hw[layer])
        both = jnp.concatenate([high, low], axis=1)
        wide[layer] = jnp.concatenate([both, both], axis=0)
    high, low = split(jnp.broadcast_to(ow[...], (height, width)))
    wide_out = jnp.concatenate(
        [jnp.concatenate([high, high], axis=1), jnp.concatenate([low, low], axis=1)], axis=0
    )
    turn = jnp.concatenate([freq[...], freq[...]], axis=1)
    half = freq.shape[1]

    def index_rows(count):
        return lax.broadcasted_iota(jnp.int32, (count, 2 * half), 0)

    def wave(t):
        t = (t - jnp.floor(t + 0.5)) * TWO_PI
        return jnp.sin(t), jnp.cos(t)

    quarter = (lax.broadcasted_iota(jnp.int32, (1, 2 * half), 1) >= half).astype(f32) * 0.25
    at_z = (index_rows(cz).astype(f32) + 0.5) / float(cz)
    sin_v, cos_v = wave(at_z * turn[2:3])
    padded_cy = -(-cy // 8) * 8
    at_y = ((gy * (rows // CF) - 1 + index_rows(padded_cy)).astype(f32) + 0.5) / float(total_cy)
    turn_y = at_y * turn[1:2]
    pick = (
        lax.broadcasted_iota(jnp.int32, (cz, height), 1) // CF
        == lax.broadcasted_iota(jnp.int32, (cz, height), 0)
    ).astype(f32)
    bias_out = ob[0, 0]

    def cells(ix, _):
        index_x = gx * (planes // CF) - 1 + ix
        inside_x = jnp.where((index_x >= 0) & (index_x < total_cx), 1.0, 0.0).astype(f32)
        at_x = (index_x.astype(f32) + 0.5) / float(total_cx)
        sin_u, cos_u = wave(turn_y + (at_x * turn[0:1] + quarter))
        hidden = jnp.concatenate(
            [sin_u[j : j + 1] * cos_v + cos_u[j : j + 1] * sin_v for j in range(cy)], axis=0
        )
        for layer in range(layers):
            lhs = jnp.concatenate(split(hidden), axis=1)
            out = jnp.dot(lhs, wide[layer], preferred_element_type=f32)
            mixed = out[:, :width] + out[:, width:] + hb[layer : layer + 1, :]
            hidden = mixed / (1.0 + jnp.exp(jnp.minimum(-mixed, 80.0)))
        lhs = jnp.concatenate(split(hidden), axis=1)
        out = lax.dot_general(
            lhs, wide_out, (((1,), (1,)), ((), ())), preferred_element_type=f32
        )
        spread = (out[:, :height] + out[:, height:]).reshape(cy, cz, height)
        logits = jnp.sum(spread * pick[None], axis=1) + bias_out
        coarse = 1.0 / (1.0 + jnp.exp(jnp.minimum(-logits, 80.0)))
        for j in range(cy):
            up[ix, CF * j : CF * j + CF, :] = jnp.broadcast_to(coarse[j : j + 1], (CF, height))
        inside = inside_y * inside_x
        for base, values in ((0, up[ix] * inside), (2, inside)):
            beside = up_z(values) + down_z(values)
            w2, w3 = 2.0 - math.sqrt(2.0), 2.0 - math.sqrt(3.0)
            one = values + w2 * beside
            two = w2 * values + w3 * beside
            filt[base, ix] = 2.0 * values + beside + up_y(one) + down_y(one)
            filt[base + 1, ix] = one + up_y(two) + down_y(two)
        return 0

    lax.fori_loop(0, cx, cells, 0)

    def filtered(i, _):
        here, back, ahead = (i + 1) // CF, i // CF, (i + 2) // CF
        top = filt[0, here] + filt[1, back] + filt[1, ahead]
        bottom = filt[2, here] + filt[3, back] + filt[3, ahead]
        value = top / jnp.maximum(bottom, 0.5)
        index_x = gx * (planes // CF) - 1 + here
        inside_x = jnp.where((index_x >= 0) & (index_x < total_cx), 1.0, 0.0).astype(f32)
        ye[i] = (0.02 + 0.98 * value * value * value) * (inside_y * inside_x)

        @pl.when((i >= HALO + 1) & (i < HALO + 1 + planes))
        def _():
            dens[i - HALO - 1] = value[CF : CF + rows]

        return 0

    lax.fori_loop(0, deep + 1, filtered, 0)

    count = nodes.shape[1]
    flat = nodes[...]
    local_x = flat[0:1] - gx * planes + HALO
    local_y = flat[1:2] - gy * rows + CF
    near = (local_x >= 0) & (local_x < deep) & (local_y >= 0) & (local_y < tall)
    place = jnp.where(near, local_x * tall + local_y, -1)
    hit_z = lax.broadcasted_iota(jnp.int32, (height, count), 0) == flat[2:3]
    pieces = [[], [], []]
    for c in range(3):
        rest = loads[c : c + 1, :]
        for term in range(3):
            high = rest.astype(bf16).astype(f32)
            pieces[term].append(jnp.where(hit_z, high, 0.0).astype(bf16))
            rest = rest - high
    table = jnp.concatenate(pieces[0] + pieces[1] + pieces[2], axis=0)
    group = 4

    def place_loads(g, _):
        here = g * (group * tall) + lax.broadcasted_iota(jnp.int32, (group * tall, count), 0)
        hit = jnp.where(here == place, 1.0, 0.0).astype(bf16)
        out = lax.dot_general(hit, table, (((1,), (1,)), ((), ())), preferred_element_type=f32)
        for c in range(3):
            parts = [out[:, (3 * t + c) * height : (3 * t + c + 1) * height] for t in range(3)]
            z_s[c, pl.ds(g * group, group)] = ((parts[2] + parts[1]) + parts[0]).reshape(
                group, tall, height
            )
        return 0

    lax.fori_loop(0, deep // group, place_loads, 0)

    for copy, (dx, dy) in copies:
        pl.when(there(dx, dy))(copy.wait_send)
        pl.when(there(-dx, -dy))(copy.wait_recv)

    edge = CF - HALO
    for ref in (force, free_s):
        ref[:, :, :edge, :] = jnp.zeros((3, deep, edge, height), f32)
        ref[:, :, tall - edge :, :] = jnp.zeros((3, deep, edge, height), f32)
    own = slice(CF, CF + rows)
    force[:, HALO : HALO + planes, own] = bf[...]
    free_s[:, HALO : HALO + planes, own] = 1.0 - fx[...].astype(f32)
    for side in range(2):
        first = 0 if side == 0 else deep - HALO
        force[:, first : first + HALO, own] = xb[side]
        free_s[:, first : first + HALO, own] = 1.0 - xf[side].astype(f32)
        start = edge if side == 0 else CF + rows
        for c in range(3):
            span = slice(HALO * c, HALO * c + HALO)
            for ref, which in ((force, 0), (free_s, 1)):
                ref[c, HALO : HALO + planes, start : start + HALO] = yh[side, :, which, span]
                for other in range(2):
                    begin = 0 if other == 0 else deep - HALO
                    ref[c, begin : begin + HALO, start : start + HALO] = ch[
                        other, side, :, which, span
                    ]
    node_row = gy * rows - CF + row
    in_y = ((node_row >= 0) & (node_row < ny * rows)).astype(f32)

    def own_plane(m):
        return jnp.where((m >= HALO) & (m < HALO + planes), 1.0, 0.0).astype(f32)

    def begin(m, total):
        node_x = gx * planes - HALO + m
        in_x = jnp.where((node_x >= 0) & (node_x < nx * planes), 1.0, 0.0).astype(f32)
        s = ye[m] + ye[m + 1]
        s = s + down_y(s)
        s = s + down_z(s)
        inv = 1.0 / jnp.maximum(DIAG * s, 1e-4)
        inv_s[m] = inv
        counted = own_row * own_plane(m)
        inside = in_y * in_x
        part = jnp.zeros(plane, f32)
        for c in range(3):
            free = free_s[c, m] * inside
            free_s[c, m] = free
            rhs = free * (force[c, m] + z_s[c, m])
            z0 = rhs * inv
            z_s[c, m] = z0
            part = part + rhs * z0
        return total + fold(part * counted)

    zero = jnp.zeros((8, height), f32)
    sum_a = lax.fori_loop(0, deep, begin, zero)

    def element_forces(src, e):
        modes = []
        for c in range(3):
            low, high = src[c, e], src[c, e + 1]
            by = {}
            for name_x, v in (("S", low + high), ("D", high - low)):
                w = up_y(v)
                for name_y, t in (("S", v + w), ("D", w - v)):
                    u = up_z(t)
                    if name_x + name_y != "SS":
                        by[name_x + name_y + "S"] = t + u
                    by[name_x + name_y + "D"] = u - t
            modes.append(by)
        x, y, z = modes
        y1 = ye[e + 1] * (1.0 / 16.0)
        y3 = y1 * (1.0 / 3.0)
        out = ({}, {}, {})
        trace = LAM * (x["DSS"] + y["SDS"] + z["SSD"])
        out[0]["DSS"] = y1 * (trace + (2 * MU) * x["DSS"])
        out[1]["SDS"] = y1 * (trace + (2 * MU) * y["SDS"])
        out[2]["SSD"] = y1 * (trace + (2 * MU) * z["SSD"])
        ym = y1 * MU
        out[0]["SDS"] = out[1]["DSS"] = ym * (x["SDS"] + y["DSS"])
        out[0]["SSD"] = out[2]["DSS"] = ym * (x["SSD"] + z["DSS"])
        out[1]["SSD"] = out[2]["SDS"] = ym * (y["SSD"] + z["SDS"])
        t = LAM * (y["DDS"] + z["DSD"])
        out[1]["DDS"] = y3 * (t + (3 * MU) * y["DDS"])
        out[2]["DSD"] = y3 * (t + (3 * MU) * z["DSD"])
        t = LAM * (x["DDS"] + z["SDD"])
        out[0]["DDS"] = y3 * (t + (3 * MU) * x["DDS"])
        out[2]["SDD"] = y3 * (t + (3 * MU) * z["SDD"])
        t = LAM * (x["DSD"] + y["SDD"])
        out[0]["DSD"] = y3 * (t + (3 * MU) * x["DSD"])
        out[1]["SDD"] = y3 * (t + (3 * MU) * y["SDD"])
        ym = y3 * MU
        p, q, r = y["DSD"], z["DDS"], x["SDD"]
        out[1]["DSD"] = ym * ((p + q) + (r + p))
        out[2]["DDS"] = ym * ((p + q) + (r + q))
        out[0]["SDD"] = ym * ((r + q) + (r + p))
        y9 = y1 * ((LAM + 4.0 * MU) / 9.0)
        for c in range(3):
            out[c]["DDD"] = y9 * modes[c]["DDD"]
        lows, highs = [], []
        for c in range(3):
            by_x = []
            for name_x in "SD":
                by_y = []
                for name_y in "SD":
                    d = out[c][name_x + name_y + "D"]
                    if name_x + name_y == "SS":
                        by_y.append(down_z(d) - d)
                    else:
                        s = out[c][name_x + name_y + "S"]
                        by_y.append((s - d) + down_z(s + d))
                s, d = by_y
                by_x.append((s - d) + down_y(s + d))
            s, d = by_x
            lows.append(s - d)
            highs.append(s + d)
        return lows, highs

    def first(e, carry):
        c0, c1, c2, sum_b, sum_c = carry
        lows, highs = element_forces(z_s, e)
        inv = inv_s[e]
        counted = own_row * own_plane(e)
        part_b = jnp.zeros(plane, f32)
        part_c = jnp.zeros(plane, f32)
        for c, before in enumerate((c0, c1, c2)):
            w = free_s[c, e] * (before + lows[c])
            q = w * inv
            q_s[c, e] = q
            part_b = part_b + w * z_s[c, e]
            part_c = part_c + w * q
        return (*highs, sum_b + fold(part_b * counted), sum_c + fold(part_c * counted))

    blank = jnp.zeros(plane, f32)
    *_, sum_b, sum_c = lax.fori_loop(0, deep - 1, first, (blank, blank, blank, zero, zero))

    def second(e, carry):
        c0, c1, c2, sum_d = carry
        lows, highs = element_forces(q_s, e)
        counted = own_row * own_plane(e)
        part = jnp.zeros(plane, f32)
        for c, before in enumerate((c0, c1, c2)):
            part = part + free_s[c, e] * (before + lows[c]) * q_s[c, e]
        return (*highs, sum_d + fold(part * counted))

    *_, sum_d = lax.fori_loop(1, HALO + planes, second, (blank, blank, blank, zero))
    mine[...] = jnp.zeros_like(mine)
    for index, value in enumerate((sum_a, sum_b, sum_c, sum_d)):
        mine[index : index + 1, :] = jnp.sum(value, axis=0, keepdims=True)

    def exchange(src, dst, size, base, where):
        moves = []
        for k in range(1, size):
            move = pltpu.make_async_remote_copy(
                src_ref=src,
                dst_ref=dst.at[k - 1],
                send_sem=sum_send.at[base + k - 1],
                recv_sem=sum_recv.at[base + k - 1],
                device_id=where(k),
                device_id_type=MESH,
            )
            move.start()
            moves.append(move)
        for move in moves:
            move.wait()

    exchange(mine, along, nx, 0, lambda k: at(k, 0))
    part[...] = mine[...] + jnp.sum(along[...], axis=0)
    exchange(part, across, ny, nx - 1, lambda k: at(0, k))
    total = jnp.sum(part[...] + jnp.sum(across[...], axis=0), axis=1, keepdims=True)
    a, b, c, d = (total[i : i + 1] for i in range(4))
    alpha = a / b
    next_rz = a - 2.0 * alpha * b + alpha * alpha * c
    beta = next_rz / a
    bent = b - 2.0 * alpha * c + alpha * alpha * d
    energy = bent + 2.0 * beta * (b - alpha * c) + beta * beta * b
    alpha_next = next_rz / energy
    on_z = jnp.broadcast_to(alpha + alpha_next * (1.0 + beta), (rows, height))
    on_q = jnp.broadcast_to(alpha_next * alpha, (rows, height))

    def finish(i, _):
        for k in range(3):
            x_out[k, i] = on_z * z_s[k, i + HALO, own] - on_q * q_s[k, i + HALO, own]
        return 0

    lax.fori_loop(0, planes, finish, 0)


def per_device(bf, fx, nodes, loads, freq, hw, hb, ow, ob):
    nx, ny = lax.axis_size("gx"), lax.axis_size("gy")
    _, planes, rows, height = bf.shape
    shape = jax.ShapeDtypeStruct
    halo = (2, 3, HALO, rows, height)
    packed = (2, planes, 2, 8, height)
    corner = (2, 2, HALO, 2, 8, height)
    cx, tall, deep = planes // CF + 2, rows + 2 * CF, planes + 2 * HALO
    width = hw.shape[2]
    field = pltpu.VMEM((3, deep, tall, height), f32)
    far = pl.BlockSpec(memory_space=pl.ANY)
    tile = (8, height)
    return pl.pallas_call(
        whole_kernel,
        out_shape=[shape(bf.shape, f32), shape(bf.shape[1:], f32)],
        in_specs=[far] * 2 + [FULL] * 6 + [pl.BlockSpec(memory_space=pltpu.SMEM)],
        out_specs=[FULL] * 2,
        scratch_shapes=[
            pltpu.VMEM(bf.shape, f32),
            pltpu.VMEM(fx.shape, jnp.int32),
            pltpu.VMEM(halo, f32),
            pltpu.VMEM(halo, jnp.int32),
            pltpu.VMEM(packed, f32),
            pltpu.VMEM(corner, f32),
            pltpu.VMEM(packed, f32),
            pltpu.VMEM((nx - 1, *tile), f32),
            pltpu.VMEM((ny - 1, *tile), f32),
            pltpu.VMEM(tile, f32),
            pltpu.VMEM(tile, f32),
            pltpu.VMEM((hw.shape[0], 2 * width, 2 * width), bf16),
            pltpu.VMEM((cx, tall, height), f32),
            pltpu.VMEM((4, cx, tall, height), f32),
            pltpu.VMEM((deep + 1, tall, height), f32),
            pltpu.VMEM((deep, tall, height), f32),
            field,
            field,
            field,
            field,
            pltpu.SemaphoreType.DMA((6,)),
            pltpu.SemaphoreType.DMA((10,)),
            pltpu.SemaphoreType.DMA((10,)),
            pltpu.SemaphoreType.DMA((nx + ny - 2,)),
            pltpu.SemaphoreType.DMA((nx + ny - 2,)),
        ],
        compiler_params=pltpu.CompilerParams(
            collective_id=0, has_side_effects=True, vmem_limit_bytes=50 << 20
        ),
    )(bf, fx, nodes.T, loads, freq, hw, hb, ow.reshape(1, -1), ob.reshape(1, 1))


def solution(mesh):
    grid = P(None, "gx", "gy", None)
    return jax.shard_map(
        per_device,
        mesh=mesh,
        in_specs=(grid, grid, P(), P(), P(), P(), P(), P(), P()),
        out_specs=(grid, P("gx", "gy", None)),
        check_vma=False,
    )
```

```python
import functools
import math

import jax
import jax.numpy as jnp
from jax import lax
from jax.experimental import pallas as pl
from jax.experimental.pallas import tpu as pltpu
from jax.sharding import PartitionSpec as P

MESH = pl.DeviceIdType.MESH
CF = 4
HALO = 2
f32 = jnp.float32
bf16 = jnp.bfloat16
POISSON = 0.3
LAM = POISSON / ((1.0 + POISSON) * (1.0 - 2.0 * POISSON))
MU = 1.0 / (2.0 * (1.0 + POISSON))
TWO_PI = 2.0 * math.pi
DIAG = ((LAM + 4.0 * MU) * (1.0 + 2.0 / 3.0 + 1.0 / 9.0)) / 16.0
FULL = pl.BlockSpec(memory_space=pltpu.VMEM)


def split(value):
    high = value.astype(bf16)
    return high, (value - high.astype(f32)).astype(bf16)


def whole_kernel(
    bf_far, fx_far, nodes_far, loads_far, freq_far, hw_far, hb_far, ow_far, ob,
    x_out, dens,
    nodes, loads, freq, hw, hb, ow, bf, fx, xb, xf, yh, ch, ys, along, across, mine, part,
    wide, up, filt, ye, inv_s, force, free_s, z_s, q_s,
    modes_s, held, ready, local, send, recv, sum_send, sum_recv,
):
    gx, gy = lax.axis_index("gx"), lax.axis_index("gy")
    nx, ny = lax.axis_size("gx"), lax.axis_size("gy")
    planes, rows, height = bf.shape[1], bf.shape[2], bf.shape[3]

    def at(dx, dy):
        return (lax.rem(gx + dx + nx, nx), lax.rem(gy + dy + ny, ny))

    barrier = pltpu.get_barrier_semaphore()
    partners = [at(dx, dy) for dx in (-1, 1) for dy in (-1, 1)]
    partners += [at(k, 0) for k in range(1, nx)] + [at(0, k) for k in range(1, ny)]
    for partner in partners:
        pl.semaphore_signal(barrier, inc=1, device_id=partner, device_id_type=MESH)
    fetches = []
    for c in range(3):
        for far, near, index in ((bf_far, bf, c), (fx_far, fx, 3 + c)):
            fetch = pltpu.make_async_copy(far.at[c], near.at[c], local.at[index])
            fetch.start()
            fetches.append(fetch)
    smalls = []
    few = (freq_far, hw_far, hb_far, ow_far, nodes_far, loads_far)
    for index, (far, near) in enumerate(zip(few, (freq, hw, hb, ow, nodes, loads))):
        fetch = pltpu.make_async_copy(far, near, local.at[6 + index])
        fetch.start()
        smalls.append(fetch)
    def there(dx, dy):
        ok = None
        for d, here, count in ((dx, gx, nx), (dy, gy, ny)):
            if d:
                one = here > 0 if d < 0 else here < count - 1
                ok = one if ok is None else ok & one
        return ok

    copies = []
    landings = []

    def launch(src, dst, step):
        index = len(copies)
        copy = pltpu.make_async_remote_copy(
            src_ref=src,
            dst_ref=dst,
            send_sem=send.at[index],
            recv_sem=recv.at[index],
            device_id=at(*step),
            device_id_type=MESH,
        )
        copies.append((copy, step))
        landings.append(dst)
        pl.when(there(*step))(copy.start)

    pl.semaphore_wait(barrier, len(partners))
    for side in range(2):
        near = pl.ds(0 if side == 0 else planes - HALO, HALO)
        launch(bf_far.at[:, near], xb.at[1 - side], (2 * side - 1, 0))
        launch(fx_far.at[:, near], xf.at[1 - side], (2 * side - 1, 0))
    for fetch in fetches:
        fetch.wait()
    for side in range(2):
        begin_row = 0 if side == 0 else rows - HALO
        for c in range(3):
            span = slice(HALO * c, HALO * c + HALO)
            ys[side, :, 0, span, :] = bf[c, :, begin_row : begin_row + HALO, :]
            ys[side, :, 1, span, :] = 1.0 - fx[c, :, begin_row : begin_row + HALO, :].astype(f32)
        ys[side, :, :, 3 * HALO :, :] = jnp.zeros((planes, 2, 8 - 3 * HALO, height), f32)
    for side in range(2):
        launch(ys.at[side], yh.at[1 - side], (0, 2 * side - 1))
        near = pl.ds(0 if side == 0 else planes - HALO, HALO)
        for other in range(2):
            launch(
                ys.at[other, near], ch.at[1 - side, 1 - other], (2 * side - 1, 2 * other - 1)
            )

    for fetch in smalls:
        fetch.wait()
    cx, cy, cz = planes // CF + 2, rows // CF + 2, height // CF
    tall = cy * CF
    deep = planes + 2 * HALO
    total_cx, total_cy = nx * (planes // CF), ny * (rows // CF)
    plane = (tall, height)
    lane = lax.broadcasted_iota(jnp.int32, plane, 1)
    row = lax.broadcasted_iota(jnp.int32, plane, 0)
    own_row = ((row >= CF) & (row < CF + rows)).astype(f32)
    cell_row = gy * rows - CF + row
    inside_y = ((cell_row >= 0) & (cell_row < ny * rows)).astype(f32)

    def up_z(v):
        return jnp.where(lane < height - 1, pltpu.roll(v, height - 1, 1), 0.0)

    def down_z(v):
        return jnp.where(lane > 0, pltpu.roll(v, 1, 1), 0.0)

    def up_y(v):
        return pltpu.roll(v, tall - 1, 0)

    def down_y(v):
        return pltpu.roll(v, 1, 0)

    def fold(v):
        return jnp.sum(v.reshape(tall // 8, 8, height), axis=0)

    layers, width = hw.shape[0], hw.shape[2]
    for layer in range(layers):
        high, low = split(hw[layer])
        both = jnp.concatenate([high, low], axis=1)
        wide[layer] = jnp.concatenate([both, both], axis=0)
    high, low = split(jnp.broadcast_to(ow[...], (height, width)))
    wide_out = jnp.concatenate(
        [jnp.concatenate([high, high], axis=1), jnp.concatenate([low, low], axis=1)], axis=0
    )
    turn = jnp.concatenate([freq[...], freq[...]], axis=1)
    half = freq.shape[1]

    def index_rows(count):
        return lax.broadcasted_iota(jnp.int32, (count, 2 * half), 0)

    def wave(t):
        t = (t - jnp.floor(t + 0.5)) * TWO_PI
        return jnp.sin(t), jnp.cos(t)

    quarter = (lax.broadcasted_iota(jnp.int32, (1, 2 * half), 1) >= half).astype(f32) * 0.25
    at_z = (index_rows(cz).astype(f32) + 0.5) / float(cz)
    sin_v, cos_v = wave(at_z * turn[2:3])
    padded_cy = -(-cy // 8) * 8
    at_y = ((gy * (rows // CF) - 1 + index_rows(padded_cy)).astype(f32) + 0.5) / float(total_cy)
    turn_y = at_y * turn[1:2]
    pick = (
        lax.broadcasted_iota(jnp.int32, (cz, height), 1) // CF
        == lax.broadcasted_iota(jnp.int32, (cz, height), 0)
    ).astype(f32)
    bias_out = ob[0, 0]

    def cells(ix, _):
        index_x = gx * (planes // CF) - 1 + ix
        inside_x = jnp.where((index_x >= 0) & (index_x < total_cx), 1.0, 0.0).astype(f32)
        at_x = (index_x.astype(f32) + 0.5) / float(total_cx)
        sin_u, cos_u = wave(turn_y + (at_x * turn[0:1] + quarter))
        hidden = jnp.concatenate(
            [sin_u[j : j + 1] * cos_v + cos_u[j : j + 1] * sin_v for j in range(cy)], axis=0
        )
        for layer in range(layers):
            lhs = jnp.concatenate(split(hidden), axis=1)
            out = jnp.dot(lhs, wide[layer], preferred_element_type=f32)
            mixed = out[:, :width] + out[:, width:] + hb[layer : layer + 1, :]
            hidden = mixed * pl.reciprocal(1.0 + jnp.exp(jnp.minimum(-mixed, 80.0)))
        lhs = jnp.concatenate(split(hidden), axis=1)
        out = lax.dot_general(
            lhs, wide_out, (((1,), (1,)), ((), ())), preferred_element_type=f32
        )
        spread = (out[:, :height] + out[:, height:]).reshape(cy, cz, height)
        logits = jnp.sum(spread * pick[None], axis=1) + bias_out
        coarse = 1.0 / (1.0 + jnp.exp(jnp.minimum(-logits, 80.0)))
        for j in range(cy):
            up[ix, CF * j : CF * j + CF, :] = jnp.broadcast_to(coarse[j : j + 1], (CF, height))
        inside = inside_y * inside_x
        for base, values in ((0, up[ix] * inside), (2, inside)):
            beside = up_z(values) + down_z(values)
            w2, w3 = 2.0 - math.sqrt(2.0), 2.0 - math.sqrt(3.0)
            one = values + w2 * beside
            two = w2 * values + w3 * beside
            filt[base, ix] = 2.0 * values + beside + up_y(one) + down_y(one)
            filt[base + 1, ix] = one + up_y(two) + down_y(two)
        return 0

    lax.fori_loop(0, cx, cells, 0)

    def filtered(i, _):
        here, back, ahead = (i + 1) // CF, i // CF, (i + 2) // CF
        top = filt[0, here] + filt[1, back] + filt[1, ahead]
        bottom = filt[2, here] + filt[3, back] + filt[3, ahead]
        value = top / jnp.maximum(bottom, 0.5)
        index_x = gx * (planes // CF) - 1 + here
        inside_x = jnp.where((index_x >= 0) & (index_x < total_cx), 1.0, 0.0).astype(f32)
        ye[i] = (0.02 + 0.98 * value * value * value) * (inside_y * inside_x)

        @pl.when((i >= HALO + 1) & (i < HALO + 1 + planes))
        def _():
            dens[i - HALO - 1] = value[CF : CF + rows]

        return 0

    lax.fori_loop(0, deep + 1, filtered, 0)

    count = nodes.shape[1]
    flat = nodes[...]
    local_x = flat[0:1] - gx * planes + HALO
    local_y = flat[1:2] - gy * rows + CF
    near = (local_x >= 0) & (local_x < deep) & (local_y >= 0) & (local_y < tall)
    place = jnp.where(near, local_x * tall + local_y, -1)
    hit_z = lax.broadcasted_iota(jnp.int32, (height, count), 0) == flat[2:3]
    pieces = [[], [], []]
    for c in range(3):
        rest = loads[c : c + 1, :]
        for term in range(3):
            high = rest.astype(bf16).astype(f32)
            pieces[term].append(jnp.where(hit_z, high, 0.0).astype(bf16))
            rest = rest - high
    table = jnp.concatenate(pieces[0] + pieces[1] + pieces[2], axis=0)
    group = 4

    def place_loads(g, _):
        here = g * (group * tall) + lax.broadcasted_iota(jnp.int32, (group * tall, count), 0)
        hit = jnp.where(here == place, 1.0, 0.0).astype(bf16)
        out = lax.dot_general(hit, table, (((1,), (1,)), ((), ())), preferred_element_type=f32)
        for c in range(3):
            parts = [out[:, (3 * t + c) * height : (3 * t + c + 1) * height] for t in range(3)]
            z_s[c, pl.ds(g * group, group)] = ((parts[2] + parts[1]) + parts[0]).reshape(
                group, tall, height
            )
        return 0

    lax.fori_loop(0, deep // group, place_loads, 0)

    def clear(ref):
        ref[...] = jnp.zeros(ref.shape, ref.dtype)

    for (copy, (dx, dy)), landing in zip(copies, landings):
        pl.when(there(dx, dy))(copy.wait_send)
        pl.when(there(-dx, -dy))(copy.wait_recv)
        pl.when(jnp.logical_not(there(-dx, -dy)))(functools.partial(clear, landing))

    edge = CF - HALO
    for ref in (force, free_s):
        ref[:, :, :edge, :] = jnp.zeros((3, deep, edge, height), f32)
        ref[:, :, tall - edge :, :] = jnp.zeros((3, deep, edge, height), f32)
    own = slice(CF, CF + rows)
    force[:, HALO : HALO + planes, own] = bf[...]
    free_s[:, HALO : HALO + planes, own] = 1.0 - fx[...].astype(f32)
    for side in range(2):
        first = 0 if side == 0 else deep - HALO
        force[:, first : first + HALO, own] = xb[side]
        free_s[:, first : first + HALO, own] = 1.0 - xf[side].astype(f32)
        start = edge if side == 0 else CF + rows
        for c in range(3):
            span = slice(HALO * c, HALO * c + HALO)
            for ref, which in ((force, 0), (free_s, 1)):
                ref[c, HALO : HALO + planes, start : start + HALO] = yh[side, :, which, span]
                for other in range(2):
                    begin = 0 if other == 0 else deep - HALO
                    ref[c, begin : begin + HALO, start : start + HALO] = ch[
                        other, side, :, which, span
                    ]
    node_row = gy * rows - CF + row
    in_y = ((node_row >= 0) & (node_row < ny * rows)).astype(f32)

    def own_plane(m):
        return jnp.where((m >= HALO) & (m < HALO + planes), 1.0, 0.0).astype(f32)

    def begin(m, total):
        node_x = gx * planes - HALO + m
        in_x = jnp.where((node_x >= 0) & (node_x < nx * planes), 1.0, 0.0).astype(f32)
        s = ye[m] + ye[m + 1]
        s = s + down_y(s)
        s = s + down_z(s)
        inv = 1.0 / jnp.maximum(DIAG * s, 1e-4)
        inv_s[m] = inv
        counted = own_row * own_plane(m)
        inside = in_y * in_x
        part = jnp.zeros(plane, f32)
        for c in range(3):
            free = free_s[c, m] * inside
            free_s[c, m] = free
            rhs = free * (force[c, m] + z_s[c, m])
            z0 = rhs * inv
            z_s[c, m] = z0
            part = part + rhs * z0
        return total + fold(part * counted)

    zero = jnp.zeros((8, height), f32)
    sum_a = lax.fori_loop(0, deep, begin, zero)

    kinds = ("SS", "SD", "DS", "DD")

    def transform(src, m):
        slot = lax.rem(m, 2)
        for c in range(3):
            v = src[c, m]
            w = up_y(v)
            for k, t in ((0, v + w), (2, w - v)):
                u = up_z(t)
                modes_s[slot, 4 * c + k] = t + u
                modes_s[slot, 4 * c + k + 1] = u - t

    def mode_forces(e, span):
        below, above = lax.rem(e, 2), lax.rem(e + 1, 2)
        modes = []
        for c in range(3):
            by = {}
            for k, kind in enumerate(kinds):
                low, high = modes_s[below, 4 * c + k, span], modes_s[above, 4 * c + k, span]
                if k:
                    by["S" + kind] = low + high
                by["D" + kind] = high - low
            modes.append(by)
        x, y, z = modes
        y1 = ye[e + 1, span] * (1.0 / 16.0)
        y3 = y1 * (1.0 / 3.0)
        out = ({}, {}, {})
        trace = LAM * (x["DSS"] + y["SDS"] + z["SSD"])
        out[0]["DSS"] = y1 * (trace + (2 * MU) * x["DSS"])
        out[1]["SDS"] = y1 * (trace + (2 * MU) * y["SDS"])
        out[2]["SSD"] = y1 * (trace + (2 * MU) * z["SSD"])
        ym = y1 * MU
        out[0]["SDS"] = out[1]["DSS"] = ym * (x["SDS"] + y["DSS"])
        out[0]["SSD"] = out[2]["DSS"] = ym * (x["SSD"] + z["DSS"])
        out[1]["SSD"] = out[2]["SDS"] = ym * (y["SSD"] + z["SDS"])
        t = LAM * (y["DDS"] + z["DSD"])
        out[1]["DDS"] = y3 * (t + (3 * MU) * y["DDS"])
        out[2]["DSD"] = y3 * (t + (3 * MU) * z["DSD"])
        t = LAM * (x["DDS"] + z["SDD"])
        out[0]["DDS"] = y3 * (t + (3 * MU) * x["DDS"])
        out[2]["SDD"] = y3 * (t + (3 * MU) * z["SDD"])
        t = LAM * (x["DSD"] + y["SDD"])
        out[0]["DSD"] = y3 * (t + (3 * MU) * x["DSD"])
        out[1]["SDD"] = y3 * (t + (3 * MU) * y["SDD"])
        ym = y3 * MU
        p, q, r = y["DSD"], z["DDS"], x["SDD"]
        out[1]["DSD"] = ym * ((p + q) + (r + p))
        out[2]["DDS"] = ym * ((p + q) + (r + q))
        out[0]["SDD"] = ym * ((r + q) + (r + p))
        y9 = y1 * ((LAM + 4.0 * MU) / 9.0)
        for c in range(3):
            out[c]["DDD"] = y9 * modes[c]["DDD"]
        for c in range(3):
            for k, kind in enumerate(kinds):
                d = out[c]["D" + kind]
                if k:
                    t = out[c]["S" + kind]
                    lower, upper = t - d, t + d
                else:
                    lower, upper = -d, d
                ready[4 * c + k, span] = held[4 * c + k, span] + lower
                held[4 * c + k, span] = upper

    def node_forces(src, e):
        transform(src, e + 1)
        for r in range(tall // 8):
            mode_forces(e, slice(8 * r, 8 * r + 8))
        forces = []
        for c in range(3):
            by_y = []
            for k in (0, 2):
                t, d = ready[4 * c + k], ready[4 * c + k + 1]
                by_y.append((t - d) + down_z(t + d))
            t, d = by_y
            forces.append((t - d) + down_y(t + d))
        return forces

    def start_forces(src, e):
        transform(src, e)
        held[...] = jnp.zeros_like(held)

    def first(e, carry):
        sum_b, sum_c = carry
        forces = node_forces(z_s, e)
        inv = inv_s[e]
        counted = own_row * own_plane(e)
        part_b = jnp.zeros(plane, f32)
        part_c = jnp.zeros(plane, f32)
        for c in range(3):
            w = free_s[c, e] * forces[c]
            q = w * inv
            q_s[c, e] = q
            part_b = part_b + w * z_s[c, e]
            part_c = part_c + w * q
        return sum_b + fold(part_b * counted), sum_c + fold(part_c * counted)

    start_forces(z_s, 0)
    sum_b, sum_c = lax.fori_loop(0, deep - 1, first, (zero, zero))

    def second(e, sum_d):
        forces = node_forces(q_s, e)
        counted = own_row * own_plane(e)
        part = jnp.zeros(plane, f32)
        for c in range(3):
            part = part + free_s[c, e] * forces[c] * q_s[c, e]
        return sum_d + fold(part * counted)

    start_forces(q_s, 1)
    sum_d = lax.fori_loop(1, HALO + planes, second, zero)
    mine[...] = jnp.zeros_like(mine)
    for index, value in enumerate((sum_a, sum_b, sum_c, sum_d)):
        mine[index : index + 1, :] = jnp.sum(value, axis=0, keepdims=True)

    def exchange(src, dst, size, base, where):
        moves = []
        for k in range(1, size):
            move = pltpu.make_async_remote_copy(
                src_ref=src,
                dst_ref=dst.at[k - 1],
                send_sem=sum_send.at[base + k - 1],
                recv_sem=sum_recv.at[base + k - 1],
                device_id=where(k),
                device_id_type=MESH,
            )
            move.start()
            moves.append(move)
        for move in moves:
            move.wait()

    exchange(mine, along, nx, 0, lambda k: at(k, 0))
    part[...] = mine[...] + jnp.sum(along[...], axis=0)
    exchange(part, across, ny, nx - 1, lambda k: at(0, k))
    total = jnp.sum(part[...] + jnp.sum(across[...], axis=0), axis=1, keepdims=True)
    a, b, c, d = (total[i : i + 1] for i in range(4))
    alpha = a / b
    next_rz = a - 2.0 * alpha * b + alpha * alpha * c
    beta = next_rz / a
    bent = b - 2.0 * alpha * c + alpha * alpha * d
    energy = bent + 2.0 * beta * (b - alpha * c) + beta * beta * b
    alpha_next = next_rz / energy
    on_z = jnp.broadcast_to(alpha + alpha_next * (1.0 + beta), (rows, height))
    on_q = jnp.broadcast_to(alpha_next * alpha, (rows, height))

    def finish(i, _):
        for k in range(3):
            x_out[k, i] = on_z * z_s[k, i + HALO, own] - on_q * q_s[k, i + HALO, own]
        return 0

    lax.fori_loop(0, planes, finish, 0)


def per_device(bf, fx, nodes, loads, freq, hw, hb, ow, ob):
    nx, ny = lax.axis_size("gx"), lax.axis_size("gy")
    _, planes, rows, height = bf.shape
    shape = jax.ShapeDtypeStruct
    halo = (2, 3, HALO, rows, height)
    packed = (2, planes, 2, 8, height)
    corner = (2, 2, HALO, 2, 8, height)
    cx, tall, deep = planes // CF + 2, rows + 2 * CF, planes + 2 * HALO
    width = hw.shape[2]
    field = pltpu.VMEM((3, deep, tall, height), f32)
    far = pl.BlockSpec(memory_space=pl.ANY)
    tile = (8, height)
    return pl.pallas_call(
        whole_kernel,
        out_shape=[shape(bf.shape, f32), shape(bf.shape[1:], f32)],
        in_specs=[far] * 8 + [pl.BlockSpec(memory_space=pltpu.SMEM)],
        out_specs=[FULL] * 2,
        scratch_shapes=[
            pltpu.VMEM((nodes.shape[1], nodes.shape[0]), jnp.int32),
            pltpu.VMEM(loads.shape, f32),
            pltpu.VMEM(freq.shape, f32),
            pltpu.VMEM(hw.shape, f32),
            pltpu.VMEM(hb.shape, f32),
            pltpu.VMEM((1, width), f32),
            pltpu.VMEM(bf.shape, f32),
            pltpu.VMEM(fx.shape, jnp.int32),
            pltpu.VMEM(halo, f32),
            pltpu.VMEM(halo, jnp.int32),
            pltpu.VMEM(packed, f32),
            pltpu.VMEM(corner, f32),
            pltpu.VMEM(packed, f32),
            pltpu.VMEM((nx - 1, *tile), f32),
            pltpu.VMEM((ny - 1, *tile), f32),
            pltpu.VMEM(tile, f32),
            pltpu.VMEM(tile, f32),
            pltpu.VMEM((hw.shape[0], 2 * width, 2 * width), bf16),
            pltpu.VMEM((cx, tall, height), f32),
            pltpu.VMEM((4, cx, tall, height), f32),
            pltpu.VMEM((deep + 1, tall, height), f32),
            pltpu.VMEM((deep, tall, height), f32),
            field,
            field,
            field,
            field,
            pltpu.VMEM((2, 12, tall, height), f32),
            pltpu.VMEM((12, tall, height), f32),
            pltpu.VMEM((12, tall, height), f32),
            pltpu.SemaphoreType.DMA((12,)),
            pltpu.SemaphoreType.DMA((10,)),
            pltpu.SemaphoreType.DMA((10,)),
            pltpu.SemaphoreType.DMA((nx + ny - 2,)),
            pltpu.SemaphoreType.DMA((nx + ny - 2,)),
        ],
        compiler_params=pltpu.CompilerParams(
            collective_id=0, has_side_effects=True, vmem_limit_bytes=64 << 20
        ),
    )(bf, fx, nodes.T, loads, freq, hw, hb, ow.reshape(1, -1), ob.reshape(1, 1))


def solution(mesh):
    grid = P(None, "gx", "gy", None)
    return jax.shard_map(
        per_device,
        mesh=mesh,
        in_specs=(grid, grid, P(), P(), P(), P(), P(), P(), P()),
        out_specs=(grid, P("gx", "gy", None)),
        check_vma=False,
    )
```

```python
import functools
import math

import jax
import jax.numpy as jnp
from jax import lax
from jax.experimental import pallas as pl
from jax.experimental.pallas import tpu as pltpu
from jax.sharding import PartitionSpec as P

MESH = pl.DeviceIdType.MESH
CF = 4
HALO = 2
f32 = jnp.float32
bf16 = jnp.bfloat16
POISSON = 0.3
LAM = POISSON / ((1.0 + POISSON) * (1.0 - 2.0 * POISSON))
MU = 1.0 / (2.0 * (1.0 + POISSON))
TWO_PI = 2.0 * math.pi
DIAG = ((LAM + 4.0 * MU) * (1.0 + 2.0 / 3.0 + 1.0 / 9.0)) / 16.0
FULL = pl.BlockSpec(memory_space=pltpu.VMEM)


def split(value):
    high = value.astype(bf16)
    return high, (value - high.astype(f32)).astype(bf16)


def whole_kernel(
    bf_far, fx_far, nodes_far, loads_far, freq_far, hw_far, hb_far, ow_far, ob,
    x_out, dens,
    nodes, loads, freq, hw, hb, ow, bf, fx, xb, xf, yh, ch, ys, along, across, mine, part,
    wide, up, filt, ye, inv_s, force, free_s, z_s, q_s,
    modes_s, held, ready, saved, local, send, recv, sum_send, sum_recv,
):
    gx, gy = lax.axis_index("gx"), lax.axis_index("gy")
    nx, ny = lax.axis_size("gx"), lax.axis_size("gy")
    planes, rows, height = bf.shape[1], bf.shape[2], bf.shape[3]

    def at(dx, dy):
        return (lax.rem(gx + dx + nx, nx), lax.rem(gy + dy + ny, ny))

    barrier = pltpu.get_barrier_semaphore()
    partners = [at(dx, dy) for dx in (-1, 1) for dy in (-1, 1)]
    partners += [at(k, 0) for k in range(1, nx)] + [at(0, k) for k in range(1, ny)]
    for partner in partners:
        pl.semaphore_signal(barrier, inc=1, device_id=partner, device_id_type=MESH)
    fetches = []
    for c in range(3):
        for far, near, index in ((bf_far, bf, c), (fx_far, fx, 3 + c)):
            fetch = pltpu.make_async_copy(far.at[c], near.at[c], local.at[index])
            fetch.start()
            fetches.append(fetch)
    smalls = []
    few = (freq_far, hw_far, hb_far, ow_far, nodes_far, loads_far)
    for index, (far, near) in enumerate(zip(few, (freq, hw, hb, ow, nodes, loads))):
        fetch = pltpu.make_async_copy(far, near, local.at[6 + index])
        fetch.start()
        smalls.append(fetch)
    def there(dx, dy):
        ok = None
        for d, here, count in ((dx, gx, nx), (dy, gy, ny)):
            if d:
                one = here > 0 if d < 0 else here < count - 1
                ok = one if ok is None else ok & one
        return ok

    copies = []
    landings = []

    def launch(src, dst, step):
        index = len(copies)
        copy = pltpu.make_async_remote_copy(
            src_ref=src,
            dst_ref=dst,
            send_sem=send.at[index],
            recv_sem=recv.at[index],
            device_id=at(*step),
            device_id_type=MESH,
        )
        copies.append((copy, step))
        landings.append(dst)
        pl.when(there(*step))(copy.start)

    pl.semaphore_wait(barrier, len(partners))
    for side in range(2):
        near = pl.ds(0 if side == 0 else planes - HALO, HALO)
        launch(bf_far.at[:, near], xb.at[1 - side], (2 * side - 1, 0))
        launch(fx_far.at[:, near], xf.at[1 - side], (2 * side - 1, 0))
    for fetch in fetches:
        fetch.wait()
    for side in range(2):
        begin_row = 0 if side == 0 else rows - HALO
        for c in range(3):
            span = slice(HALO * c, HALO * c + HALO)
            ys[side, :, 0, span, :] = bf[c, :, begin_row : begin_row + HALO, :]
            ys[side, :, 1, span, :] = 1.0 - fx[c, :, begin_row : begin_row + HALO, :].astype(f32)
        ys[side, :, :, 3 * HALO :, :] = jnp.zeros((planes, 2, 8 - 3 * HALO, height), f32)
    for side in range(2):
        launch(ys.at[side], yh.at[1 - side], (0, 2 * side - 1))
        near = pl.ds(0 if side == 0 else planes - HALO, HALO)
        for other in range(2):
            launch(
                ys.at[other, near], ch.at[1 - side, 1 - other], (2 * side - 1, 2 * other - 1)
            )

    for fetch in smalls:
        fetch.wait()
    cx, cy, cz = planes // CF + 2, rows // CF + 2, height // CF
    tall = cy * CF
    deep = planes + 2 * HALO
    total_cx, total_cy = nx * (planes // CF), ny * (rows // CF)
    plane = (tall, height)
    lane = lax.broadcasted_iota(jnp.int32, plane, 1)
    row = lax.broadcasted_iota(jnp.int32, plane, 0)
    own_row = ((row >= CF) & (row < CF + rows)).astype(f32)
    cell_row = gy * rows - CF + row
    inside_y = ((cell_row >= 0) & (cell_row < ny * rows)).astype(f32)

    def up_z(v):
        return jnp.where(lane < height - 1, pltpu.roll(v, height - 1, 1), 0.0)

    def down_z(v):
        return jnp.where(lane > 0, pltpu.roll(v, 1, 1), 0.0)

    def up_y(v):
        return pltpu.roll(v, tall - 1, 0)

    def down_y(v):
        return pltpu.roll(v, 1, 0)

    def fold(v):
        return jnp.sum(v.reshape(tall // 8, 8, height), axis=0)

    layers, width = hw.shape[0], hw.shape[2]
    for layer in range(layers):
        high, low = split(hw[layer])
        both = jnp.concatenate([high, low], axis=1)
        wide[layer] = jnp.concatenate([both, both], axis=0)
    high, low = split(jnp.broadcast_to(ow[...], (height, width)))
    wide_out = jnp.concatenate(
        [jnp.concatenate([high, high], axis=1), jnp.concatenate([low, low], axis=1)], axis=0
    )
    turn = jnp.concatenate([freq[...], freq[...]], axis=1)
    half = freq.shape[1]

    def index_rows(count):
        return lax.broadcasted_iota(jnp.int32, (count, 2 * half), 0)

    def wave(t):
        t = (t - jnp.floor(t + 0.5)) * TWO_PI
        return jnp.sin(t), jnp.cos(t)

    quarter = (lax.broadcasted_iota(jnp.int32, (1, 2 * half), 1) >= half).astype(f32) * 0.25
    at_z = (index_rows(cz).astype(f32) + 0.5) / float(cz)
    sin_v, cos_v = wave(at_z * turn[2:3])
    padded_cy = -(-cy // 8) * 8
    at_y = ((gy * (rows // CF) - 1 + index_rows(padded_cy)).astype(f32) + 0.5) / float(total_cy)
    turn_y = at_y * turn[1:2]
    pick = (
        lax.broadcasted_iota(jnp.int32, (cz, height), 1) // CF
        == lax.broadcasted_iota(jnp.int32, (cz, height), 0)
    ).astype(f32)
    bias_out = ob[0]

    def cells(ix, _):
        index_x = gx * (planes // CF) - 1 + ix
        inside_x = jnp.where((index_x >= 0) & (index_x < total_cx), 1.0, 0.0).astype(f32)
        at_x = (index_x.astype(f32) + 0.5) / float(total_cx)
        sin_u, cos_u = wave(turn_y + (at_x * turn[0:1] + quarter))
        hidden = jnp.concatenate(
            [sin_u[j : j + 1] * cos_v + cos_u[j : j + 1] * sin_v for j in range(cy)], axis=0
        )
        for layer in range(layers):
            lhs = jnp.concatenate(split(hidden), axis=1)
            out = jnp.dot(lhs, wide[layer], preferred_element_type=f32)
            mixed = out[:, :width] + out[:, width:] + hb[layer : layer + 1, :]
            hidden = mixed * pl.reciprocal(1.0 + jnp.exp(jnp.minimum(-mixed, 80.0)))
        lhs = jnp.concatenate(split(hidden), axis=1)
        out = lax.dot_general(
            lhs, wide_out, (((1,), (1,)), ((), ())), preferred_element_type=f32
        )
        spread = (out[:, :height] + out[:, height:]).reshape(cy, cz, height)
        logits = jnp.sum(spread * pick[None], axis=1) + bias_out
        coarse = 1.0 / (1.0 + jnp.exp(jnp.minimum(-logits, 80.0)))
        for j in range(cy):
            up[ix, CF * j : CF * j + CF, :] = jnp.broadcast_to(coarse[j : j + 1], (CF, height))
        inside = inside_y * inside_x
        for base, values in ((0, up[ix] * inside), (2, inside)):
            beside = up_z(values) + down_z(values)
            w2, w3 = 2.0 - math.sqrt(2.0), 2.0 - math.sqrt(3.0)
            one = values + w2 * beside
            two = w2 * values + w3 * beside
            filt[base, ix] = 2.0 * values + beside + up_y(one) + down_y(one)
            filt[base + 1, ix] = one + up_y(two) + down_y(two)
        return 0

    lax.fori_loop(0, cx, cells, 0)

    def filtered(i, _):
        here, back, ahead = (i + 1) // CF, i // CF, (i + 2) // CF
        top = filt[0, here] + filt[1, back] + filt[1, ahead]
        bottom = filt[2, here] + filt[3, back] + filt[3, ahead]
        value = top / jnp.maximum(bottom, 0.5)
        index_x = gx * (planes // CF) - 1 + here
        inside_x = jnp.where((index_x >= 0) & (index_x < total_cx), 1.0, 0.0).astype(f32)
        ye[i] = (0.02 + 0.98 * value * value * value) * (inside_y * inside_x)

        @pl.when((i >= HALO + 1) & (i < HALO + 1 + planes))
        def _():
            dens[i - HALO - 1] = value[CF : CF + rows]

        return 0

    lax.fori_loop(0, deep + 1, filtered, 0)

    count = nodes.shape[1]
    flat = nodes[...]
    local_x = flat[0:1] - gx * planes + HALO
    local_y = flat[1:2] - gy * rows + CF
    near = (local_x >= 0) & (local_x < deep) & (local_y >= 0) & (local_y < tall)
    place = jnp.where(near, local_x * tall + local_y, -1)
    hit_z = lax.broadcasted_iota(jnp.int32, (height, count), 0) == flat[2:3]
    pieces = [[], [], []]
    for c in range(3):
        rest = loads[c : c + 1, :]
        for term in range(3):
            high = rest.astype(bf16).astype(f32)
            pieces[term].append(jnp.where(hit_z, high, 0.0).astype(bf16))
            rest = rest - high
    table = jnp.concatenate(pieces[0] + pieces[1] + pieces[2], axis=0)
    group = 4

    def place_loads(g, _):
        here = g * (group * tall) + lax.broadcasted_iota(jnp.int32, (group * tall, count), 0)
        hit = jnp.where(here == place, 1.0, 0.0).astype(bf16)
        out = lax.dot_general(hit, table, (((1,), (1,)), ((), ())), preferred_element_type=f32)
        for c in range(3):
            parts = [out[:, (3 * t + c) * height : (3 * t + c + 1) * height] for t in range(3)]
            z_s[c, pl.ds(g * group, group)] = ((parts[2] + parts[1]) + parts[0]).reshape(
                group, tall, height
            )
        return 0

    lax.fori_loop(0, deep // group, place_loads, 0)

    def clear(ref):
        ref[...] = jnp.zeros(ref.shape, ref.dtype)

    def settle(chosen):
        for index in chosen:
            (copy, (dx, dy)), landing = copies[index], landings[index]
            pl.when(there(dx, dy))(copy.wait_send)
            pl.when(there(-dx, -dy))(copy.wait_recv)
            pl.when(jnp.logical_not(there(-dx, -dy)))(functools.partial(clear, landing))

    beside_y = [i for i, (_, step) in enumerate(copies) if step[0] == 0]
    beside_x = [i for i, (_, step) in enumerate(copies) if step[0] != 0]
    settle(beside_y)

    edge = CF - HALO
    for ref in (force, free_s):
        ref[:, :, :edge, :] = jnp.zeros((3, deep, edge, height), f32)
        ref[:, :, tall - edge :, :] = jnp.zeros((3, deep, edge, height), f32)
    own = slice(CF, CF + rows)
    force[:, HALO : HALO + planes, own] = bf[...]
    free_s[:, HALO : HALO + planes, own] = 1.0 - fx[...].astype(f32)
    def halo_rows(side):
        start = edge if side == 0 else CF + rows
        return slice(start, start + HALO)

    def halo_planes(side):
        start = 0 if side == 0 else deep - HALO
        return slice(start, start + HALO)

    for side in range(2):
        for c in range(3):
            span = slice(HALO * c, HALO * c + HALO)
            for ref, which in ((force, 0), (free_s, 1)):
                ref[c, HALO : HALO + planes, halo_rows(side)] = yh[side, :, which, span]

    def place_x_halos():
        for side in range(2):
            force[:, halo_planes(side), own] = xb[side]
            free_s[:, halo_planes(side), own] = 1.0 - xf[side].astype(f32)
            for c in range(3):
                span = slice(HALO * c, HALO * c + HALO)
                for ref, which in ((force, 0), (free_s, 1)):
                    for other in range(2):
                        ref[c, halo_planes(other), halo_rows(side)] = ch[
                            other, side, :, which, span
                        ]

    node_row = gy * rows - CF + row
    in_y = ((node_row >= 0) & (node_row < ny * rows)).astype(f32)

    def own_plane(m):
        return jnp.where((m >= HALO) & (m < HALO + planes), 1.0, 0.0).astype(f32)

    def begin(m, total):
        node_x = gx * planes - HALO + m
        in_x = jnp.where((node_x >= 0) & (node_x < nx * planes), 1.0, 0.0).astype(f32)
        s = ye[m] + ye[m + 1]
        s = s + down_y(s)
        s = s + down_z(s)
        inv = 1.0 / jnp.maximum(DIAG * s, 1e-4)
        inv_s[m] = inv
        counted = own_row * own_plane(m)
        inside = in_y * in_x
        part = jnp.zeros(plane, f32)
        for c in range(3):
            free = free_s[c, m] * inside
            free_s[c, m] = free
            rhs = free * (force[c, m] + z_s[c, m])
            z0 = rhs * inv
            z_s[c, m] = z0
            part = part + rhs * z0
        return total + fold(part * counted)

    zero = jnp.zeros((8, height), f32)
    sum_a = lax.fori_loop(HALO, HALO + planes, begin, zero)

    kinds = ("SS", "SD", "DS", "DD")

    def transform(src, m):
        slot = lax.rem(m, 2)
        for c in range(3):
            v = src[c, m]
            w = up_y(v)
            for k, t in ((0, v + w), (2, w - v)):
                u = up_z(t)
                modes_s[slot, 4 * c + k] = t + u
                modes_s[slot, 4 * c + k + 1] = u - t

    def mode_forces(e, span):
        below, above = lax.rem(e, 2), lax.rem(e + 1, 2)
        modes = []
        for c in range(3):
            by = {}
            for k, kind in enumerate(kinds):
                low, high = modes_s[below, 4 * c + k, span], modes_s[above, 4 * c + k, span]
                if k:
                    by["S" + kind] = low + high
                by["D" + kind] = high - low
            modes.append(by)
        x, y, z = modes
        y1 = ye[e + 1, span] * (1.0 / 16.0)
        y3 = y1 * (1.0 / 3.0)
        out = ({}, {}, {})
        trace = LAM * (x["DSS"] + y["SDS"] + z["SSD"])
        out[0]["DSS"] = y1 * (trace + (2 * MU) * x["DSS"])
        out[1]["SDS"] = y1 * (trace + (2 * MU) * y["SDS"])
        out[2]["SSD"] = y1 * (trace + (2 * MU) * z["SSD"])
        ym = y1 * MU
        out[0]["SDS"] = out[1]["DSS"] = ym * (x["SDS"] + y["DSS"])
        out[0]["SSD"] = out[2]["DSS"] = ym * (x["SSD"] + z["DSS"])
        out[1]["SSD"] = out[2]["SDS"] = ym * (y["SSD"] + z["SDS"])
        t = LAM * (y["DDS"] + z["DSD"])
        out[1]["DDS"] = y3 * (t + (3 * MU) * y["DDS"])
        out[2]["DSD"] = y3 * (t + (3 * MU) * z["DSD"])
        t = LAM * (x["DDS"] + z["SDD"])
        out[0]["DDS"] = y3 * (t + (3 * MU) * x["DDS"])
        out[2]["SDD"] = y3 * (t + (3 * MU) * z["SDD"])
        t = LAM * (x["DSD"] + y["SDD"])
        out[0]["DSD"] = y3 * (t + (3 * MU) * x["DSD"])
        out[1]["SDD"] = y3 * (t + (3 * MU) * y["SDD"])
        ym = y3 * MU
        p, q, r = y["DSD"], z["DDS"], x["SDD"]
        out[1]["DSD"] = ym * ((p + q) + (r + p))
        out[2]["DDS"] = ym * ((p + q) + (r + q))
        out[0]["SDD"] = ym * ((r + q) + (r + p))
        y9 = y1 * ((LAM + 4.0 * MU) / 9.0)
        for c in range(3):
            out[c]["DDD"] = y9 * modes[c]["DDD"]
        for c in range(3):
            for k, kind in enumerate(kinds):
                d = out[c]["D" + kind]
                if k:
                    t = out[c]["S" + kind]
                    lower, upper = t - d, t + d
                else:
                    lower, upper = -d, d
                ready[4 * c + k, span] = held[4 * c + k, span] + lower
                held[4 * c + k, span] = upper

    def advance(src, e):
        transform(src, e + 1)
        for r in range(tall // 8):
            mode_forces(e, slice(8 * r, 8 * r + 8))

    def gather():
        forces = []
        for c in range(3):
            by_y = []
            for k in (0, 2):
                t, d = ready[4 * c + k], ready[4 * c + k + 1]
                by_y.append((t - d) + down_z(t + d))
            t, d = by_y
            forces.append((t - d) + down_y(t + d))
        return forces

    def start_forces(src, e):
        transform(src, e)
        held[...] = jnp.zeros_like(held)

    def first_node(e, carry):
        sum_b, sum_c = carry
        forces = gather()
        inv = inv_s[e]
        counted = own_row * own_plane(e)
        part_b = jnp.zeros(plane, f32)
        part_c = jnp.zeros(plane, f32)
        for c in range(3):
            w = free_s[c, e] * forces[c]
            q = w * inv
            q_s[c, e] = q
            part_b = part_b + w * z_s[c, e]
            part_c = part_c + w * q
        return sum_b + fold(part_b * counted), sum_c + fold(part_c * counted)

    def first(e, carry):
        advance(z_s, e)
        return first_node(e, carry)

    start_forces(z_s, HALO)
    advance(z_s, HALO)
    saved[...] = ready[...]
    last = HALO + planes - 1
    carry = lax.fori_loop(HALO + 1, last, first, (zero, zero))
    settle(beside_x)
    place_x_halos()
    lax.fori_loop(0, HALO, begin, zero)
    lax.fori_loop(deep - HALO, deep, begin, zero)
    carry = lax.fori_loop(last, last + 2, first, carry)
    start_forces(z_s, 0)
    advance(z_s, 0)
    carry = lax.fori_loop(1, HALO, first, carry)
    ready[...] = held[...] + saved[...]
    sum_b, sum_c = first_node(HALO, carry)

    def second(e, sum_d):
        advance(q_s, e)
        forces = gather()
        counted = own_row * own_plane(e)
        part = jnp.zeros(plane, f32)
        for c in range(3):
            part = part + free_s[c, e] * forces[c] * q_s[c, e]
        return sum_d + fold(part * counted)

    start_forces(q_s, 1)
    sum_d = lax.fori_loop(1, HALO + planes, second, zero)
    mine[...] = jnp.zeros_like(mine)
    for index, value in enumerate((sum_a, sum_b, sum_c, sum_d)):
        mine[index : index + 1, :] = jnp.sum(value, axis=0, keepdims=True)

    def exchange(src, dst, size, base, where):
        moves = []
        for k in range(1, size):
            move = pltpu.make_async_remote_copy(
                src_ref=src,
                dst_ref=dst.at[k - 1],
                send_sem=sum_send.at[base + k - 1],
                recv_sem=sum_recv.at[base + k - 1],
                device_id=where(k),
                device_id_type=MESH,
            )
            move.start()
            moves.append(move)
        for move in moves:
            move.wait()

    exchange(mine, along, nx, 0, lambda k: at(k, 0))
    part[...] = mine[...] + jnp.sum(along[...], axis=0)
    exchange(part, across, ny, nx - 1, lambda k: at(0, k))
    total = jnp.sum(part[...] + jnp.sum(across[...], axis=0), axis=1, keepdims=True)
    a, b, c, d = (total[i : i + 1] for i in range(4))
    alpha = a / b
    next_rz = a - 2.0 * alpha * b + alpha * alpha * c
    beta = next_rz / a
    bent = b - 2.0 * alpha * c + alpha * alpha * d
    energy = bent + 2.0 * beta * (b - alpha * c) + beta * beta * b
    alpha_next = next_rz / energy
    on_z = jnp.broadcast_to(alpha + alpha_next * (1.0 + beta), (rows, height))
    on_q = jnp.broadcast_to(alpha_next * alpha, (rows, height))

    def finish(i, _):
        for k in range(3):
            x_out[k, i] = on_z * z_s[k, i + HALO, own] - on_q * q_s[k, i + HALO, own]
        return 0

    lax.fori_loop(0, planes, finish, 0)


def per_device(bf, fx, nodes, loads, freq, hw, hb, ow, ob):
    nx, ny = lax.axis_size("gx"), lax.axis_size("gy")
    _, planes, rows, height = bf.shape
    shape = jax.ShapeDtypeStruct
    halo = (2, 3, HALO, rows, height)
    packed = (2, planes, 2, 8, height)
    corner = (2, 2, HALO, 2, 8, height)
    cx, tall, deep = planes // CF + 2, rows + 2 * CF, planes + 2 * HALO
    width = hw.shape[2]
    field = pltpu.VMEM((3, deep, tall, height), f32)
    far = pl.BlockSpec(memory_space=pl.ANY)
    tile = (8, height)
    displacement, density = pl.pallas_call(
        whole_kernel,
        out_shape=[shape(bf.shape, f32), shape(bf.shape[1:], f32)],
        in_specs=[far] * 8 + [pl.BlockSpec(memory_space=pltpu.SMEM)],
        out_specs=[FULL] * 2,
        scratch_shapes=[
            pltpu.VMEM((nodes.shape[1], nodes.shape[0]), jnp.int32),
            pltpu.VMEM(loads.shape, f32),
            pltpu.VMEM(freq.shape, f32),
            pltpu.VMEM(hw.shape, f32),
            pltpu.VMEM(hb.shape, f32),
            pltpu.VMEM((1, width), f32),
            pltpu.VMEM(bf.shape, f32),
            pltpu.VMEM(fx.shape, jnp.int32),
            pltpu.VMEM(halo, f32),
            pltpu.VMEM(halo, jnp.int32),
            pltpu.VMEM(packed, f32),
            pltpu.VMEM(corner, f32),
            pltpu.VMEM(packed, f32),
            pltpu.VMEM((nx - 1, *tile), f32),
            pltpu.VMEM((ny - 1, *tile), f32),
            pltpu.VMEM(tile, f32),
            pltpu.VMEM(tile, f32),
            pltpu.VMEM((hw.shape[0], 2 * width, 2 * width), bf16),
            pltpu.VMEM((cx, tall, height), f32),
            pltpu.VMEM((4, cx, tall, height), f32),
            pltpu.VMEM((deep + 1, tall, height), f32),
            pltpu.VMEM((deep, tall, height), f32),
            field,
            field,
            field,
            field,
            pltpu.VMEM((2, 12, tall, height), f32),
            pltpu.VMEM((12, tall, height), f32),
            pltpu.VMEM((12, tall, height), f32),
            pltpu.VMEM((12, tall, height), f32),
            pltpu.SemaphoreType.DMA((12,)),
            pltpu.SemaphoreType.DMA((10,)),
            pltpu.SemaphoreType.DMA((10,)),
            pltpu.SemaphoreType.DMA((nx + ny - 2,)),
            pltpu.SemaphoreType.DMA((nx + ny - 2,)),
        ],
        compiler_params=pltpu.CompilerParams(
            collective_id=0, has_side_effects=True, vmem_limit_bytes=64 << 20
        ),
    )(bf, fx, nodes.T, loads, freq, hw, hb, ow.reshape(1, -1), ob)
    return jnp.where(fx == 0, displacement, 0.0), density


def solution(mesh):
    grid = P(None, "gx", "gy", None)
    return jax.shard_map(
        per_device,
        mesh=mesh,
        in_specs=(grid, grid, P(), P(), P(), P(), P(), P(), P()),
        out_specs=(grid, P("gx", "gy", None)),
        check_vma=False,
    )
```

```python
import functools
import math

import jax
import jax.numpy as jnp
from jax import lax
from jax.experimental import pallas as pl
from jax.experimental.pallas import tpu as pltpu
from jax.sharding import PartitionSpec as P

MESH = pl.DeviceIdType.MESH
CF = 4
HALO = 2
f32 = jnp.float32
bf16 = jnp.bfloat16
POISSON = 0.3
LAM = POISSON / ((1.0 + POISSON) * (1.0 - 2.0 * POISSON))
MU = 1.0 / (2.0 * (1.0 + POISSON))
TWO_PI = 2.0 * math.pi
DIAG = ((LAM + 4.0 * MU) * (1.0 + 2.0 / 3.0 + 1.0 / 9.0)) / 16.0
FULL = pl.BlockSpec(memory_space=pltpu.VMEM)


def split(value):
    high = value.astype(bf16)
    return high, (value - high.astype(f32)).astype(bf16)


def whole_kernel(
    bf_far, fx_far, nodes_far, loads_far, freq_far, hw_far, hb_far, ow_far, ob,
    x_out, dens,
    nodes, loads, freq, hw, hb, ow, bf, fx, xb, xf, yh, ch, ys, along, across, mine, part,
    wide, up, filt, ye, inv_s, force, free_s, z_s, q_s,
    modes_s, held, ready, saved, local, send, recv, sum_send, sum_recv,
):
    gx, gy = lax.axis_index("gx"), lax.axis_index("gy")
    nx, ny = lax.axis_size("gx"), lax.axis_size("gy")
    planes, rows, height = bf.shape[1], bf.shape[2], bf.shape[3]

    def at(dx, dy):
        return (lax.rem(gx + dx + nx, nx), lax.rem(gy + dy + ny, ny))

    barrier = pltpu.get_barrier_semaphore()
    partners = [at(dx, dy) for dx in (-1, 1) for dy in (-1, 1)]
    partners += [at(k, 0) for k in range(1, nx)] + [at(0, k) for k in range(1, ny)]
    for partner in partners:
        pl.semaphore_signal(barrier, inc=1, device_id=partner, device_id_type=MESH)
    fetches = []
    for c in range(3):
        for far, near, index in ((bf_far, bf, c), (fx_far, fx, 3 + c)):
            fetch = pltpu.make_async_copy(far.at[c], near.at[c], local.at[index])
            fetch.start()
            fetches.append(fetch)
    smalls = []
    few = (freq_far, hw_far, hb_far, ow_far, nodes_far, loads_far)
    for index, (far, near) in enumerate(zip(few, (freq, hw, hb, ow, nodes, loads))):
        fetch = pltpu.make_async_copy(far, near, local.at[6 + index])
        fetch.start()
        smalls.append(fetch)
    def there(dx, dy):
        ok = None
        for d, here, count in ((dx, gx, nx), (dy, gy, ny)):
            if d:
                one = here > 0 if d < 0 else here < count - 1
                ok = one if ok is None else ok & one
        return ok

    copies = []
    landings = []

    def launch(src, dst, step):
        index = len(copies)
        copy = pltpu.make_async_remote_copy(
            src_ref=src,
            dst_ref=dst,
            send_sem=send.at[index],
            recv_sem=recv.at[index],
            device_id=at(*step),
            device_id_type=MESH,
        )
        copies.append((copy, step))
        landings.append(dst)
        pl.when(there(*step))(copy.start)

    pl.semaphore_wait(barrier, len(partners))
    for side in range(2):
        near = pl.ds(0 if side == 0 else planes - HALO, HALO)
        launch(bf_far.at[:, near], xb.at[1 - side], (2 * side - 1, 0))
        launch(fx_far.at[:, near], xf.at[1 - side], (2 * side - 1, 0))
    for fetch in fetches:
        fetch.wait()
    for side in range(2):
        begin_row = 0 if side == 0 else rows - HALO
        for c in range(3):
            span = slice(HALO * c, HALO * c + HALO)
            ys[side, :, 0, span, :] = bf[c, :, begin_row : begin_row + HALO, :]
            ys[side, :, 1, span, :] = 1.0 - fx[c, :, begin_row : begin_row + HALO, :].astype(f32)
        ys[side, :, :, 3 * HALO :, :] = jnp.zeros((planes, 2, 8 - 3 * HALO, height), f32)
    for side in range(2):
        launch(ys.at[side], yh.at[1 - side], (0, 2 * side - 1))
        near = pl.ds(0 if side == 0 else planes - HALO, HALO)
        for other in range(2):
            launch(
                ys.at[other, near], ch.at[1 - side, 1 - other], (2 * side - 1, 2 * other - 1)
            )

    for fetch in smalls:
        fetch.wait()
    cx, cy, cz = planes // CF + 2, rows // CF + 2, height // CF
    tall = cy * CF
    deep = planes + 2 * HALO
    total_cx, total_cy = nx * (planes // CF), ny * (rows // CF)
    plane = (tall, height)
    lane = lax.broadcasted_iota(jnp.int32, plane, 1)
    row = lax.broadcasted_iota(jnp.int32, plane, 0)
    own_row = ((row >= CF) & (row < CF + rows)).astype(f32)
    cell_row = gy * rows - CF + row
    inside_y = ((cell_row >= 0) & (cell_row < ny * rows)).astype(f32)

    def up_z(v):
        return jnp.where(lane < height - 1, pltpu.roll(v, height - 1, 1), 0.0)

    def down_z(v):
        return jnp.where(lane > 0, pltpu.roll(v, 1, 1), 0.0)

    def up_y(v):
        return pltpu.roll(v, tall - 1, 0)

    def down_y(v):
        return pltpu.roll(v, 1, 0)

    def fold(v):
        return jnp.sum(v.reshape(tall // 8, 8, height), axis=0)

    layers, width = hw.shape[0], hw.shape[2]
    for layer in range(layers):
        high, low = split(hw[layer])
        both = jnp.concatenate([high, low], axis=1)
        wide[layer] = jnp.concatenate([both, both], axis=0)
    high, low = split(jnp.broadcast_to(ow[...], (height, width)))
    wide_out = jnp.concatenate(
        [jnp.concatenate([high, high], axis=1), jnp.concatenate([low, low], axis=1)], axis=0
    )
    turn = jnp.concatenate([freq[...], freq[...]], axis=1)
    half = freq.shape[1]

    def index_rows(count):
        return lax.broadcasted_iota(jnp.int32, (count, 2 * half), 0)

    def wave(t):
        t = (t - jnp.floor(t + 0.5)) * TWO_PI
        return jnp.sin(t), jnp.cos(t)

    quarter = (lax.broadcasted_iota(jnp.int32, (1, 2 * half), 1) >= half).astype(f32) * 0.25
    at_z = (index_rows(cz).astype(f32) + 0.5) / float(cz)
    sin_v, cos_v = wave(at_z * turn[2:3])
    padded_cy = -(-cy // 8) * 8
    at_y = ((gy * (rows // CF) - 1 + index_rows(padded_cy)).astype(f32) + 0.5) / float(total_cy)
    turn_y = at_y * turn[1:2]
    pick = (
        lax.broadcasted_iota(jnp.int32, (cz, height), 1) // CF
        == lax.broadcasted_iota(jnp.int32, (cz, height), 0)
    ).astype(f32)
    bias_out = ob[0]

    at_once = max(k for k in (1, 2, 3) if cx % k == 0)

    def cells(step, _):
        blocks = []
        for k in range(at_once):
            index_x = gx * (planes // CF) - 1 + step * at_once + k
            at_x = (index_x.astype(f32) + 0.5) / float(total_cx)
            sin_u, cos_u = wave(turn_y + (at_x * turn[0:1] + quarter))
            for j in range(cy):
                blocks.append(sin_u[j : j + 1] * cos_v + cos_u[j : j + 1] * sin_v)
        hidden = jnp.concatenate(blocks, axis=0)
        for layer in range(layers):
            lhs = jnp.concatenate(split(hidden), axis=1)
            out = jnp.dot(lhs, wide[layer], preferred_element_type=f32)
            mixed = out[:, :width] + out[:, width:] + hb[layer : layer + 1, :]
            hidden = mixed * pl.reciprocal(1.0 + jnp.exp(jnp.minimum(-mixed, 80.0)))
        lhs = jnp.concatenate(split(hidden), axis=1)
        out = lax.dot_general(
            lhs, wide_out, (((1,), (1,)), ((), ())), preferred_element_type=f32
        )
        spread = (out[:, :height] + out[:, height:]).reshape(at_once, cy, cz, height)
        for k in range(at_once):
            ix = step * at_once + k
            index_x = gx * (planes // CF) - 1 + ix
            inside_x = jnp.where((index_x >= 0) & (index_x < total_cx), 1.0, 0.0).astype(f32)
            logits = jnp.sum(spread[k] * pick[None], axis=1) + bias_out
            coarse = 1.0 / (1.0 + jnp.exp(jnp.minimum(-logits, 80.0)))
            for j in range(cy):
                up[ix, CF * j : CF * j + CF, :] = jnp.broadcast_to(
                    coarse[j : j + 1], (CF, height)
                )
            inside = inside_y * inside_x
            for base, values in ((0, up[ix] * inside), (2, inside)):
                beside = up_z(values) + down_z(values)
                w2, w3 = 2.0 - math.sqrt(2.0), 2.0 - math.sqrt(3.0)
                one = values + w2 * beside
                two = w2 * values + w3 * beside
                filt[base, ix] = 2.0 * values + beside + up_y(one) + down_y(one)
                filt[base + 1, ix] = one + up_y(two) + down_y(two)
        return 0

    lax.fori_loop(0, cx // at_once, cells, 0)

    def filtered(i, _):
        here, back, ahead = (i + 1) // CF, i // CF, (i + 2) // CF
        top = filt[0, here] + filt[1, back] + filt[1, ahead]
        bottom = filt[2, here] + filt[3, back] + filt[3, ahead]
        value = top / jnp.maximum(bottom, 0.5)
        index_x = gx * (planes // CF) - 1 + here
        inside_x = jnp.where((index_x >= 0) & (index_x < total_cx), 1.0, 0.0).astype(f32)
        ye[i] = (0.02 + 0.98 * value * value * value) * (inside_y * inside_x)

        @pl.when((i >= HALO + 1) & (i < HALO + 1 + planes))
        def _():
            dens[i - HALO - 1] = value[CF : CF + rows]

        return 0

    lax.fori_loop(0, deep + 1, filtered, 0, unroll=3)

    count = nodes.shape[1]
    flat = nodes[...]
    local_x = flat[0:1] - gx * planes + HALO
    local_y = flat[1:2] - gy * rows + CF
    near = (local_x >= 0) & (local_x < deep) & (local_y >= 0) & (local_y < tall)
    place = jnp.where(near, local_x * tall + local_y, -1)
    hit_z = lax.broadcasted_iota(jnp.int32, (height, count), 0) == flat[2:3]
    pieces = [[], [], []]
    for c in range(3):
        rest = loads[c : c + 1, :]
        for term in range(3):
            high = rest.astype(bf16).astype(f32)
            pieces[term].append(jnp.where(hit_z, high, 0.0).astype(bf16))
            rest = rest - high
    table = jnp.concatenate(pieces[0] + pieces[1] + pieces[2], axis=0)
    group = 4

    def place_loads(g, _):
        here = g * (group * tall) + lax.broadcasted_iota(jnp.int32, (group * tall, count), 0)
        hit = jnp.where(here == place, 1.0, 0.0).astype(bf16)
        out = lax.dot_general(hit, table, (((1,), (1,)), ((), ())), preferred_element_type=f32)
        for c in range(3):
            parts = [out[:, (3 * t + c) * height : (3 * t + c + 1) * height] for t in range(3)]
            z_s[c, pl.ds(g * group, group)] = ((parts[2] + parts[1]) + parts[0]).reshape(
                group, tall, height
            )
        return 0

    lax.fori_loop(0, deep // group, place_loads, 0)

    def clear(ref):
        ref[...] = jnp.zeros(ref.shape, ref.dtype)

    def settle(chosen):
        for index in chosen:
            (copy, (dx, dy)), landing = copies[index], landings[index]
            pl.when(there(dx, dy))(copy.wait_send)
            pl.when(there(-dx, -dy))(copy.wait_recv)
            pl.when(jnp.logical_not(there(-dx, -dy)))(functools.partial(clear, landing))

    beside_y = [i for i, (_, step) in enumerate(copies) if step[0] == 0]
    beside_x = [i for i, (_, step) in enumerate(copies) if step[0] != 0]
    settle(beside_y)

    edge = CF - HALO
    for ref in (force, free_s):
        ref[:, :, :edge, :] = jnp.zeros((3, deep, edge, height), f32)
        ref[:, :, tall - edge :, :] = jnp.zeros((3, deep, edge, height), f32)
    own = slice(CF, CF + rows)
    force[:, HALO : HALO + planes, own] = bf[...]
    free_s[:, HALO : HALO + planes, own] = 1.0 - fx[...].astype(f32)
    def halo_rows(side):
        start = edge if side == 0 else CF + rows
        return slice(start, start + HALO)

    def halo_planes(side):
        start = 0 if side == 0 else deep - HALO
        return slice(start, start + HALO)

    for side in range(2):
        for c in range(3):
            span = slice(HALO * c, HALO * c + HALO)
            for ref, which in ((force, 0), (free_s, 1)):
                ref[c, HALO : HALO + planes, halo_rows(side)] = yh[side, :, which, span]

    def place_x_halos():
        for side in range(2):
            force[:, halo_planes(side), own] = xb[side]
            free_s[:, halo_planes(side), own] = 1.0 - xf[side].astype(f32)
            for c in range(3):
                span = slice(HALO * c, HALO * c + HALO)
                for ref, which in ((force, 0), (free_s, 1)):
                    for other in range(2):
                        ref[c, halo_planes(other), halo_rows(side)] = ch[
                            other, side, :, which, span
                        ]

    node_row = gy * rows - CF + row
    in_y = ((node_row >= 0) & (node_row < ny * rows)).astype(f32)

    def own_plane(m):
        return jnp.where((m >= HALO) & (m < HALO + planes), 1.0, 0.0).astype(f32)

    def begin(m, total):
        node_x = gx * planes - HALO + m
        in_x = jnp.where((node_x >= 0) & (node_x < nx * planes), 1.0, 0.0).astype(f32)
        s = ye[m] + ye[m + 1]
        s = s + down_y(s)
        s = s + down_z(s)
        inv = 1.0 / jnp.maximum(DIAG * s, 1e-4)
        inv_s[m] = inv
        counted = own_row * own_plane(m)
        inside = in_y * in_x
        part = jnp.zeros(plane, f32)
        for c in range(3):
            free = free_s[c, m] * inside
            free_s[c, m] = free
            rhs = free * (force[c, m] + z_s[c, m])
            z0 = rhs * inv
            z_s[c, m] = z0
            part = part + rhs * z0
        return total + fold(part * counted)

    zero = jnp.zeros((8, height), f32)
    sum_a = lax.fori_loop(HALO, HALO + planes, begin, zero, unroll=2)

    kinds = ("SS", "SD", "DS", "DD")

    def transform(src, m):
        slot = lax.rem(m, 2)
        for c in range(3):
            v = src[c, m]
            w = up_y(v)
            for k, t in ((0, v + w), (2, w - v)):
                u = up_z(t)
                modes_s[slot, 4 * c + k] = t + u
                modes_s[slot, 4 * c + k + 1] = u - t

    def mode_forces(e, span):
        below, above = lax.rem(e, 2), lax.rem(e + 1, 2)
        modes = []
        for c in range(3):
            by = {}
            for k, kind in enumerate(kinds):
                low, high = modes_s[below, 4 * c + k, span], modes_s[above, 4 * c + k, span]
                if k:
                    by["S" + kind] = low + high
                by["D" + kind] = high - low
            modes.append(by)
        x, y, z = modes
        y1 = ye[e + 1, span] * (1.0 / 16.0)
        y3 = y1 * (1.0 / 3.0)
        out = ({}, {}, {})
        trace = LAM * (x["DSS"] + y["SDS"] + z["SSD"])
        out[0]["DSS"] = y1 * (trace + (2 * MU) * x["DSS"])
        out[1]["SDS"] = y1 * (trace + (2 * MU) * y["SDS"])
        out[2]["SSD"] = y1 * (trace + (2 * MU) * z["SSD"])
        ym = y1 * MU
        out[0]["SDS"] = out[1]["DSS"] = ym * (x["SDS"] + y["DSS"])
        out[0]["SSD"] = out[2]["DSS"] = ym * (x["SSD"] + z["DSS"])
        out[1]["SSD"] = out[2]["SDS"] = ym * (y["SSD"] + z["SDS"])
        t = LAM * (y["DDS"] + z["DSD"])
        out[1]["DDS"] = y3 * (t + (3 * MU) * y["DDS"])
        out[2]["DSD"] = y3 * (t + (3 * MU) * z["DSD"])
        t = LAM * (x["DDS"] + z["SDD"])
        out[0]["DDS"] = y3 * (t + (3 * MU) * x["DDS"])
        out[2]["SDD"] = y3 * (t + (3 * MU) * z["SDD"])
        t = LAM * (x["DSD"] + y["SDD"])
        out[0]["DSD"] = y3 * (t + (3 * MU) * x["DSD"])
        out[1]["SDD"] = y3 * (t + (3 * MU) * y["SDD"])
        ym = y3 * MU
        p, q, r = y["DSD"], z["DDS"], x["SDD"]
        out[1]["DSD"] = ym * ((p + q) + (r + p))
        out[2]["DDS"] = ym * ((p + q) + (r + q))
        out[0]["SDD"] = ym * ((r + q) + (r + p))
        y9 = y1 * ((LAM + 4.0 * MU) / 9.0)
        for c in range(3):
            out[c]["DDD"] = y9 * modes[c]["DDD"]
        for c in range(3):
            for k, kind in enumerate(kinds):
                d = out[c]["D" + kind]
                if k:
                    t = out[c]["S" + kind]
                    lower, upper = t - d, t + d
                else:
                    lower, upper = -d, d
                ready[4 * c + k, span] = held[4 * c + k, span] + lower
                held[4 * c + k, span] = upper

    def advance(src, e):
        transform(src, e + 1)
        for r in range(tall // 8):
            mode_forces(e, slice(8 * r, 8 * r + 8))

    def gather():
        forces = []
        for c in range(3):
            by_y = []
            for k in (0, 2):
                t, d = ready[4 * c + k], ready[4 * c + k + 1]
                by_y.append((t - d) + down_z(t + d))
            t, d = by_y
            forces.append((t - d) + down_y(t + d))
        return forces

    def start_forces(src, e):
        transform(src, e)
        held[...] = jnp.zeros_like(held)

    def first_node(e, carry):
        sum_b, sum_c = carry
        forces = gather()
        inv = inv_s[e]
        counted = own_row * own_plane(e)
        part_b = jnp.zeros(plane, f32)
        part_c = jnp.zeros(plane, f32)
        for c in range(3):
            w = free_s[c, e] * forces[c]
            q = w * inv
            q_s[c, e] = q
            part_b = part_b + w * z_s[c, e]
            part_c = part_c + w * q
        return sum_b + fold(part_b * counted), sum_c + fold(part_c * counted)

    def first(e, carry):
        advance(z_s, e)
        return first_node(e, carry)

    start_forces(z_s, HALO)
    advance(z_s, HALO)
    saved[...] = ready[...]
    last = HALO + planes - 1
    carry = lax.fori_loop(HALO + 1, last, first, (zero, zero))
    settle(beside_x)
    place_x_halos()
    lax.fori_loop(0, HALO, begin, zero)
    lax.fori_loop(deep - HALO, deep, begin, zero)
    carry = lax.fori_loop(last, last + 2, first, carry)
    start_forces(z_s, 0)
    advance(z_s, 0)
    carry = lax.fori_loop(1, HALO, first, carry)
    ready[...] = held[...] + saved[...]
    sum_b, sum_c = first_node(HALO, carry)

    def second(e, sum_d):
        advance(q_s, e)
        forces = gather()
        counted = own_row * own_plane(e)
        part = jnp.zeros(plane, f32)
        for c in range(3):
            part = part + free_s[c, e] * forces[c] * q_s[c, e]
        return sum_d + fold(part * counted)

    start_forces(q_s, 1)
    sum_d = lax.fori_loop(1, HALO + planes, second, zero)
    mine[...] = jnp.zeros_like(mine)
    for index, value in enumerate((sum_a, sum_b, sum_c, sum_d)):
        mine[index : index + 1, :] = jnp.sum(value, axis=0, keepdims=True)

    def exchange(src, dst, size, base, where):
        moves = []
        for k in range(1, size):
            move = pltpu.make_async_remote_copy(
                src_ref=src,
                dst_ref=dst.at[k - 1],
                send_sem=sum_send.at[base + k - 1],
                recv_sem=sum_recv.at[base + k - 1],
                device_id=where(k),
                device_id_type=MESH,
            )
            move.start()
            moves.append(move)
        for move in moves:
            move.wait()

    exchange(mine, along, nx, 0, lambda k: at(k, 0))
    part[...] = mine[...] + jnp.sum(along[...], axis=0)
    exchange(part, across, ny, nx - 1, lambda k: at(0, k))
    total = jnp.sum(part[...] + jnp.sum(across[...], axis=0), axis=1, keepdims=True)
    a, b, c, d = (total[i : i + 1] for i in range(4))
    alpha = a / b
    next_rz = a - 2.0 * alpha * b + alpha * alpha * c
    beta = next_rz / a
    bent = b - 2.0 * alpha * c + alpha * alpha * d
    energy = bent + 2.0 * beta * (b - alpha * c) + beta * beta * b
    alpha_next = next_rz / energy
    on_z = jnp.broadcast_to(alpha + alpha_next * (1.0 + beta), (rows, height))
    on_q = jnp.broadcast_to(alpha_next * alpha, (rows, height))

    def finish(i, _):
        for k in range(3):
            x_out[k, i] = on_z * z_s[k, i + HALO, own] - on_q * q_s[k, i + HALO, own]
        return 0

    lax.fori_loop(0, planes, finish, 0, unroll=4)


def per_device(bf, fx, nodes, loads, freq, hw, hb, ow, ob):
    nx, ny = lax.axis_size("gx"), lax.axis_size("gy")
    _, planes, rows, height = bf.shape
    shape = jax.ShapeDtypeStruct
    halo = (2, 3, HALO, rows, height)
    packed = (2, planes, 2, 8, height)
    corner = (2, 2, HALO, 2, 8, height)
    cx, tall, deep = planes // CF + 2, rows + 2 * CF, planes + 2 * HALO
    width = hw.shape[2]
    field = pltpu.VMEM((3, deep, tall, height), f32)
    far = pl.BlockSpec(memory_space=pl.ANY)
    tile = (8, height)
    displacement, density = pl.pallas_call(
        whole_kernel,
        out_shape=[shape(bf.shape, f32), shape(bf.shape[1:], f32)],
        in_specs=[far] * 8 + [pl.BlockSpec(memory_space=pltpu.SMEM)],
        out_specs=[FULL] * 2,
        scratch_shapes=[
            pltpu.VMEM((nodes.shape[1], nodes.shape[0]), jnp.int32),
            pltpu.VMEM(loads.shape, f32),
            pltpu.VMEM(freq.shape, f32),
            pltpu.VMEM(hw.shape, f32),
            pltpu.VMEM(hb.shape, f32),
            pltpu.VMEM((1, width), f32),
            pltpu.VMEM(bf.shape, f32),
            pltpu.VMEM(fx.shape, jnp.int32),
            pltpu.VMEM(halo, f32),
            pltpu.VMEM(halo, jnp.int32),
            pltpu.VMEM(packed, f32),
            pltpu.VMEM(corner, f32),
            pltpu.VMEM(packed, f32),
            pltpu.VMEM((nx - 1, *tile), f32),
            pltpu.VMEM((ny - 1, *tile), f32),
            pltpu.VMEM(tile, f32),
            pltpu.VMEM(tile, f32),
            pltpu.VMEM((hw.shape[0], 2 * width, 2 * width), bf16),
            pltpu.VMEM((cx, tall, height), f32),
            pltpu.VMEM((4, cx, tall, height), f32),
            pltpu.VMEM((deep + 1, tall, height), f32),
            pltpu.VMEM((deep, tall, height), f32),
            field,
            field,
            field,
            field,
            pltpu.VMEM((2, 12, tall, height), f32),
            pltpu.VMEM((12, tall, height), f32),
            pltpu.VMEM((12, tall, height), f32),
            pltpu.VMEM((12, tall, height), f32),
            pltpu.SemaphoreType.DMA((12,)),
            pltpu.SemaphoreType.DMA((10,)),
            pltpu.SemaphoreType.DMA((10,)),
            pltpu.SemaphoreType.DMA((nx + ny - 2,)),
            pltpu.SemaphoreType.DMA((nx + ny - 2,)),
        ],
        compiler_params=pltpu.CompilerParams(
            collective_id=0, has_side_effects=True, vmem_limit_bytes=63 << 20
        ),
    )(bf, fx, nodes.T, loads, freq, hw, hb, ow.reshape(1, -1), ob)
    return jnp.where(fx == 0, displacement, 0.0), density


def solution(mesh):
    grid = P(None, "gx", "gy", None)
    return jax.shard_map(
        per_device,
        mesh=mesh,
        in_specs=(grid, grid, P(), P(), P(), P(), P(), P(), P()),
        out_specs=(grid, P("gx", "gy", None)),
        check_vma=False,
    )
```

```python
import functools
import math

import jax
import jax.numpy as jnp
from jax import lax
from jax.experimental import pallas as pl
from jax.experimental.pallas import tpu as pltpu
from jax.sharding import PartitionSpec as P

MESH = pl.DeviceIdType.MESH
CF = 4
HALO = 2
f32 = jnp.float32
bf16 = jnp.bfloat16
POISSON = 0.3
LAM = POISSON / ((1.0 + POISSON) * (1.0 - 2.0 * POISSON))
MU = 1.0 / (2.0 * (1.0 + POISSON))
TWO_PI = 2.0 * math.pi
DIAG = ((LAM + 4.0 * MU) * (1.0 + 2.0 / 3.0 + 1.0 / 9.0)) / 16.0
FULL = pl.BlockSpec(memory_space=pltpu.VMEM)


def split(value):
    high = value.astype(bf16)
    return high, (value - high.astype(f32)).astype(bf16)


def whole_kernel(
    bf_far, fx_far, nodes_far, loads_far, freq_far, hw_far, hb_far, ow_far, ob,
    x_out, dens,
    nodes, loads, freq, hw, hb, ow, bf, fx, xb, xf, yh, ch, ys, along, across, mine, part,
    wide, up, filt, ye, inv_s, force, free_s, z_s, q_s,
    modes_s, held, ready, saved, local, send, recv, sum_send, sum_recv,
):
    gx, gy = lax.axis_index("gx"), lax.axis_index("gy")
    nx, ny = lax.axis_size("gx"), lax.axis_size("gy")
    planes, rows, height = bf.shape[1], bf.shape[2], bf.shape[3]

    def at(dx, dy):
        return (lax.rem(gx + dx + nx, nx), lax.rem(gy + dy + ny, ny))

    barrier = pltpu.get_barrier_semaphore()
    partners = [at(dx, dy) for dx in (-1, 1) for dy in (-1, 1)]
    partners += [at(k, 0) for k in range(1, nx)] + [at(0, k) for k in range(1, ny)]
    for partner in partners:
        pl.semaphore_signal(barrier, inc=1, device_id=partner, device_id_type=MESH)
    fetches = []
    for c in range(3):
        for far, near, index in ((bf_far, bf, c), (fx_far, fx, 3 + c)):
            fetch = pltpu.make_async_copy(far.at[c], near.at[c], local.at[index])
            fetch.start()
            fetches.append(fetch)
    smalls = []
    few = (freq_far, hw_far, hb_far, ow_far, nodes_far, loads_far)
    for index, (far, near) in enumerate(zip(few, (freq, hw, hb, ow, nodes, loads))):
        fetch = pltpu.make_async_copy(far, near, local.at[6 + index])
        fetch.start()
        smalls.append(fetch)
    def there(dx, dy):
        ok = None
        for d, here, count in ((dx, gx, nx), (dy, gy, ny)):
            if d:
                one = here > 0 if d < 0 else here < count - 1
                ok = one if ok is None else ok & one
        return ok

    copies = []
    landings = []

    def launch(src, dst, step):
        index = len(copies)
        copy = pltpu.make_async_remote_copy(
            src_ref=src,
            dst_ref=dst,
            send_sem=send.at[index],
            recv_sem=recv.at[index],
            device_id=at(*step),
            device_id_type=MESH,
        )
        copies.append((copy, step))
        landings.append(dst)
        pl.when(there(*step))(copy.start)

    pl.semaphore_wait(barrier, len(partners))
    for side in range(2):
        near = pl.ds(0 if side == 0 else planes - HALO, HALO)
        launch(bf_far.at[:, near], xb.at[1 - side], (2 * side - 1, 0))
        launch(fx_far.at[:, near], xf.at[1 - side], (2 * side - 1, 0))
    for fetch in fetches:
        fetch.wait()
    for side in range(2):
        begin_row = 0 if side == 0 else rows - HALO
        for c in range(3):
            span = slice(HALO * c, HALO * c + HALO)
            ys[side, :, 0, span, :] = bf[c, :, begin_row : begin_row + HALO, :]
            ys[side, :, 1, span, :] = 1.0 - fx[c, :, begin_row : begin_row + HALO, :].astype(f32)
        ys[side, :, :, 3 * HALO :, :] = jnp.zeros((planes, 2, 8 - 3 * HALO, height), f32)
    for side in range(2):
        launch(ys.at[side], yh.at[1 - side], (0, 2 * side - 1))
        near = pl.ds(0 if side == 0 else planes - HALO, HALO)
        for other in range(2):
            launch(
                ys.at[other, near], ch.at[1 - side, 1 - other], (2 * side - 1, 2 * other - 1)
            )

    for fetch in smalls:
        fetch.wait()
    cx, cy, cz = planes // CF + 2, rows // CF + 2, height // CF
    tall = cy * CF
    deep = planes + 2 * HALO
    total_cx, total_cy = nx * (planes // CF), ny * (rows // CF)
    plane = (tall, height)
    lane = lax.broadcasted_iota(jnp.int32, plane, 1)
    row = lax.broadcasted_iota(jnp.int32, plane, 0)
    own_row = ((row >= CF) & (row < CF + rows)).astype(f32)
    cell_row = gy * rows - CF + row
    inside_y = ((cell_row >= 0) & (cell_row < ny * rows)).astype(f32)

    def up_z(v):
        return jnp.where(lane < height - 1, pltpu.roll(v, height - 1, 1), 0.0)

    def down_z(v):
        return jnp.where(lane > 0, pltpu.roll(v, 1, 1), 0.0)

    def up_y(v):
        return pltpu.roll(v, tall - 1, 0)

    def down_y(v):
        return pltpu.roll(v, 1, 0)

    def fold(v):
        return jnp.sum(v.reshape(tall // 8, 8, height), axis=0)

    layers, width = hw.shape[0], hw.shape[2]
    for layer in range(layers):
        high, low = split(hw[layer])
        both = jnp.concatenate([high, low], axis=1)
        wide[layer] = jnp.concatenate([both, both], axis=0)
    high, low = split(jnp.broadcast_to(ow[...], (height, width)))
    wide_out = jnp.concatenate(
        [jnp.concatenate([high, high], axis=1), jnp.concatenate([low, low], axis=1)], axis=0
    )
    turn = jnp.concatenate([freq[...], freq[...]], axis=1)
    half = freq.shape[1]

    def index_rows(count):
        return lax.broadcasted_iota(jnp.int32, (count, 2 * half), 0)

    def wave(t):
        t = (t - jnp.floor(t + 0.5)) * TWO_PI
        return jnp.sin(t), jnp.cos(t)

    quarter = (lax.broadcasted_iota(jnp.int32, (1, 2 * half), 1) >= half).astype(f32) * 0.25
    at_z = (index_rows(cz).astype(f32) + 0.5) / float(cz)
    sin_v, cos_v = wave(at_z * turn[2:3])
    padded_cy = -(-cy // 8) * 8
    at_y = ((gy * (rows // CF) - 1 + index_rows(padded_cy)).astype(f32) + 0.5) / float(total_cy)
    turn_y = at_y * turn[1:2]
    pick = (
        lax.broadcasted_iota(jnp.int32, (cz, height), 1) // CF
        == lax.broadcasted_iota(jnp.int32, (cz, height), 0)
    ).astype(f32)
    bias_out = ob[0]

    at_once = max(k for k in (1, 2, 3) if cx % k == 0)

    def cells(step, _):
        blocks = []
        for k in range(at_once):
            index_x = gx * (planes // CF) - 1 + step * at_once + k
            at_x = (index_x.astype(f32) + 0.5) / float(total_cx)
            sin_u, cos_u = wave(turn_y + (at_x * turn[0:1] + quarter))
            for j in range(cy):
                blocks.append(sin_u[j : j + 1] * cos_v + cos_u[j : j + 1] * sin_v)
        hidden = jnp.concatenate(blocks, axis=0)
        for layer in range(layers):
            lhs = jnp.concatenate(split(hidden), axis=1)
            out = jnp.dot(lhs, wide[layer], preferred_element_type=f32)
            mixed = out[:, :width] + out[:, width:] + hb[layer : layer + 1, :]
            hidden = mixed * pl.reciprocal(1.0 + jnp.exp(jnp.minimum(-mixed, 80.0)))
        lhs = jnp.concatenate(split(hidden), axis=1)
        out = lax.dot_general(
            lhs, wide_out, (((1,), (1,)), ((), ())), preferred_element_type=f32
        )
        spread = (out[:, :height] + out[:, height:]).reshape(at_once, cy, cz, height)
        for k in range(at_once):
            ix = step * at_once + k
            index_x = gx * (planes // CF) - 1 + ix
            inside_x = jnp.where((index_x >= 0) & (index_x < total_cx), 1.0, 0.0).astype(f32)
            logits = jnp.sum(spread[k] * pick[None], axis=1) + bias_out
            coarse = 1.0 / (1.0 + jnp.exp(jnp.minimum(-logits, 80.0)))
            for j in range(cy):
                up[ix, CF * j : CF * j + CF, :] = jnp.broadcast_to(
                    coarse[j : j + 1], (CF, height)
                )
            inside = inside_y * inside_x
            for base, values in ((0, up[ix] * inside), (2, inside)):
                beside = up_z(values) + down_z(values)
                w2, w3 = 2.0 - math.sqrt(2.0), 2.0 - math.sqrt(3.0)
                one = values + w2 * beside
                two = w2 * values + w3 * beside
                filt[base, ix] = 2.0 * values + beside + up_y(one) + down_y(one)
                filt[base + 1, ix] = one + up_y(two) + down_y(two)
        return 0

    lax.fori_loop(0, cx // at_once, cells, 0)

    def filtered(i, _):
        here, back, ahead = (i + 1) // CF, i // CF, (i + 2) // CF
        top = filt[0, here] + filt[1, back] + filt[1, ahead]
        bottom = filt[2, here] + filt[3, back] + filt[3, ahead]
        value = top / jnp.maximum(bottom, 0.5)
        index_x = gx * (planes // CF) - 1 + here
        inside_x = jnp.where((index_x >= 0) & (index_x < total_cx), 1.0, 0.0).astype(f32)
        ye[i] = (0.02 + 0.98 * value * value * value) * (inside_y * inside_x)

        @pl.when((i >= HALO + 1) & (i < HALO + 1 + planes))
        def _():
            dens[i - HALO - 1] = value[CF : CF + rows]

        return 0

    lax.fori_loop(0, deep + 1, filtered, 0, unroll=3)

    count = nodes.shape[1]
    flat = nodes[...]
    local_x = flat[0:1] - gx * planes + HALO
    local_y = flat[1:2] - gy * rows + CF
    near = (local_x >= 0) & (local_x < deep) & (local_y >= 0) & (local_y < tall)
    place = jnp.where(near, local_x * tall + local_y, -1)
    hit_z = lax.broadcasted_iota(jnp.int32, (height, count), 0) == flat[2:3]
    pieces = [[], [], []]
    for c in range(3):
        rest = loads[c : c + 1, :]
        for term in range(3):
            high = rest.astype(bf16).astype(f32)
            pieces[term].append(jnp.where(hit_z, high, 0.0).astype(bf16))
            rest = rest - high
    table = jnp.concatenate(pieces[0] + pieces[1] + pieces[2], axis=0)
    group = 4

    def place_loads(g, _):
        here = g * (group * tall) + lax.broadcasted_iota(jnp.int32, (group * tall, count), 0)
        hit = jnp.where(here == place, 1.0, 0.0).astype(bf16)
        out = lax.dot_general(hit, table, (((1,), (1,)), ((), ())), preferred_element_type=f32)
        for c in range(3):
            parts = [out[:, (3 * t + c) * height : (3 * t + c + 1) * height] for t in range(3)]
            z_s[c, pl.ds(g * group, group)] = ((parts[2] + parts[1]) + parts[0]).reshape(
                group, tall, height
            )
        return 0

    lax.fori_loop(0, deep // group, place_loads, 0)

    def clear(ref):
        ref[...] = jnp.zeros(ref.shape, ref.dtype)

    def settle(chosen):
        for index in chosen:
            (copy, (dx, dy)), landing = copies[index], landings[index]
            pl.when(there(dx, dy))(copy.wait_send)
            pl.when(there(-dx, -dy))(copy.wait_recv)
            pl.when(jnp.logical_not(there(-dx, -dy)))(functools.partial(clear, landing))

    beside_y = [i for i, (_, step) in enumerate(copies) if step[0] == 0]
    beside_x = [i for i, (_, step) in enumerate(copies) if step[0] != 0]
    settle(beside_y)

    edge = CF - HALO
    for ref in (force, free_s):
        ref[:, :, :edge, :] = jnp.zeros((3, deep, edge, height), f32)
        ref[:, :, tall - edge :, :] = jnp.zeros((3, deep, edge, height), f32)
    own = slice(CF, CF + rows)
    force[:, HALO : HALO + planes, own] = bf[...]
    free_s[:, HALO : HALO + planes, own] = 1.0 - fx[...].astype(f32)
    def halo_rows(side):
        start = edge if side == 0 else CF + rows
        return slice(start, start + HALO)

    def halo_planes(side):
        start = 0 if side == 0 else deep - HALO
        return slice(start, start + HALO)

    for side in range(2):
        for c in range(3):
            span = slice(HALO * c, HALO * c + HALO)
            for ref, which in ((force, 0), (free_s, 1)):
                ref[c, HALO : HALO + planes, halo_rows(side)] = yh[side, :, which, span]

    def place_x_halos():
        for side in range(2):
            force[:, halo_planes(side), own] = xb[side]
            free_s[:, halo_planes(side), own] = 1.0 - xf[side].astype(f32)
            for c in range(3):
                span = slice(HALO * c, HALO * c + HALO)
                for ref, which in ((force, 0), (free_s, 1)):
                    for other in range(2):
                        ref[c, halo_planes(other), halo_rows(side)] = ch[
                            other, side, :, which, span
                        ]

    node_row = gy * rows - CF + row
    in_y = ((node_row >= 0) & (node_row < ny * rows)).astype(f32)

    def own_plane(m):
        return jnp.where((m >= HALO) & (m < HALO + planes), 1.0, 0.0).astype(f32)

    def begin(m, total):
        node_x = gx * planes - HALO + m
        in_x = jnp.where((node_x >= 0) & (node_x < nx * planes), 1.0, 0.0).astype(f32)
        s = ye[m] + ye[m + 1]
        s = s + down_y(s)
        s = s + down_z(s)
        inv = 1.0 / jnp.maximum(DIAG * s, 1e-4)
        inv_s[m] = inv
        counted = own_row * own_plane(m)
        inside = in_y * in_x
        part = jnp.zeros(plane, f32)
        for c in range(3):
            free = free_s[c, m] * inside
            free_s[c, m] = free
            rhs = free * (force[c, m] + z_s[c, m])
            z0 = rhs * inv
            z_s[c, m] = z0
            part = part + rhs * z0
        return total + fold(part * counted)

    zero = jnp.zeros((8, height), f32)
    sum_a = lax.fori_loop(HALO, HALO + planes, begin, zero, unroll=2)

    kinds = ("SS", "SD", "DS", "DD")

    def transform(src, m, slot):
        for c in range(3):
            v = src[c, m]
            w = up_y(v)
            for k, t in ((0, v + w), (2, w - v)):
                u = up_z(t)
                modes_s[slot, 4 * c + k] = t + u
                modes_s[slot, 4 * c + k + 1] = u - t

    def mode_forces(e, span, below):
        above = 1 - below
        modes = []
        for c in range(3):
            by = {}
            for k, kind in enumerate(kinds):
                low, high = modes_s[below, 4 * c + k, span], modes_s[above, 4 * c + k, span]
                if k:
                    by["S" + kind] = low + high
                by["D" + kind] = high - low
            modes.append(by)
        x, y, z = modes
        y1 = ye[e + 1, span] * (1.0 / 16.0)
        y3 = y1 * (1.0 / 3.0)
        out = ({}, {}, {})
        trace = LAM * (x["DSS"] + y["SDS"] + z["SSD"])
        out[0]["DSS"] = y1 * (trace + (2 * MU) * x["DSS"])
        out[1]["SDS"] = y1 * (trace + (2 * MU) * y["SDS"])
        out[2]["SSD"] = y1 * (trace + (2 * MU) * z["SSD"])
        ym = y1 * MU
        out[0]["SDS"] = out[1]["DSS"] = ym * (x["SDS"] + y["DSS"])
        out[0]["SSD"] = out[2]["DSS"] = ym * (x["SSD"] + z["DSS"])
        out[1]["SSD"] = out[2]["SDS"] = ym * (y["SSD"] + z["SDS"])
        t = LAM * (y["DDS"] + z["DSD"])
        out[1]["DDS"] = y3 * (t + (3 * MU) * y["DDS"])
        out[2]["DSD"] = y3 * (t + (3 * MU) * z["DSD"])
        t = LAM * (x["DDS"] + z["SDD"])
        out[0]["DDS"] = y3 * (t + (3 * MU) * x["DDS"])
        out[2]["SDD"] = y3 * (t + (3 * MU) * z["SDD"])
        t = LAM * (x["DSD"] + y["SDD"])
        out[0]["DSD"] = y3 * (t + (3 * MU) * x["DSD"])
        out[1]["SDD"] = y3 * (t + (3 * MU) * y["SDD"])
        ym = y3 * MU
        p, q, r = y["DSD"], z["DDS"], x["SDD"]
        out[1]["DSD"] = ym * ((p + q) + (r + p))
        out[2]["DDS"] = ym * ((p + q) + (r + q))
        out[0]["SDD"] = ym * ((r + q) + (r + p))
        y9 = y1 * ((LAM + 4.0 * MU) / 9.0)
        for c in range(3):
            out[c]["DDD"] = y9 * modes[c]["DDD"]
        for c in range(3):
            for k, kind in enumerate(kinds):
                d = out[c]["D" + kind]
                if k:
                    t = out[c]["S" + kind]
                    lower, upper = t - d, t + d
                else:
                    lower, upper = -d, d
                ready[4 * c + k, span] = held[4 * c + k, span] + lower
                held[4 * c + k, span] = upper

    def advance(src, e, below):
        transform(src, e + 1, 1 - below)
        for r in range(tall // 8):
            mode_forces(e, slice(8 * r, 8 * r + 8), below)

    def gather():
        forces = []
        for c in range(3):
            by_y = []
            for k in (0, 2):
                t, d = ready[4 * c + k], ready[4 * c + k + 1]
                by_y.append((t - d) + down_z(t + d))
            t, d = by_y
            forces.append((t - d) + down_y(t + d))
        return forces

    def start_forces(src, e):
        transform(src, e, e % 2)
        held[...] = jnp.zeros_like(held)

    def first_node(e, carry):
        sum_b, sum_c = carry
        forces = gather()
        inv = inv_s[e]
        counted = own_row * own_plane(e)
        part_b = jnp.zeros(plane, f32)
        part_c = jnp.zeros(plane, f32)
        for c in range(3):
            w = free_s[c, e] * forces[c]
            q = w * inv
            q_s[c, e] = q
            part_b = part_b + w * z_s[c, e]
            part_c = part_c + w * q
        return sum_b + fold(part_b * counted), sum_c + fold(part_c * counted)

    def first(e, carry, below):
        advance(z_s, e, below)
        return first_node(e, carry)

    def in_pairs(body, start, stop, carry):
        def pair(i, carry):
            e = start + 2 * i
            return body(e + 1, body(e, carry, start % 2), 1 - start % 2)

        carry = lax.fori_loop(0, (stop - start) // 2, pair, carry)
        if (stop - start) % 2:
            carry = body(jnp.int32(stop - 1), carry, (stop - 1) % 2)
        return carry

    start_forces(z_s, HALO)
    advance(z_s, HALO, HALO % 2)
    saved[...] = ready[...]
    last = HALO + planes - 1
    carry = in_pairs(first, HALO + 1, last, (zero, zero))
    settle(beside_x)
    place_x_halos()
    lax.fori_loop(0, HALO, begin, zero)
    lax.fori_loop(deep - HALO, deep, begin, zero)
    carry = in_pairs(first, last, last + 2, carry)
    start_forces(z_s, 0)
    advance(z_s, 0, 0)
    carry = in_pairs(first, 1, HALO, carry)
    ready[...] = held[...] + saved[...]
    sum_b, sum_c = first_node(HALO, carry)

    def second(e, sum_d, below):
        advance(q_s, e, below)
        forces = gather()
        counted = own_row * own_plane(e)
        part = jnp.zeros(plane, f32)
        for c in range(3):
            part = part + free_s[c, e] * forces[c] * q_s[c, e]
        return sum_d + fold(part * counted)

    start_forces(q_s, 1)
    sum_d = in_pairs(second, 1, HALO + planes, zero)
    mine[...] = jnp.zeros_like(mine)
    for index, value in enumerate((sum_a, sum_b, sum_c, sum_d)):
        mine[index : index + 1, :] = jnp.sum(value, axis=0, keepdims=True)

    def exchange(src, dst, size, base, where):
        moves = []
        for k in range(1, size):
            move = pltpu.make_async_remote_copy(
                src_ref=src,
                dst_ref=dst.at[k - 1],
                send_sem=sum_send.at[base + k - 1],
                recv_sem=sum_recv.at[base + k - 1],
                device_id=where(k),
                device_id_type=MESH,
            )
            move.start()
            moves.append(move)
        for move in moves:
            move.wait()

    exchange(mine, along, nx, 0, lambda k: at(k, 0))
    part[...] = mine[...] + jnp.sum(along[...], axis=0)
    exchange(part, across, ny, nx - 1, lambda k: at(0, k))
    total = jnp.sum(part[...] + jnp.sum(across[...], axis=0), axis=1, keepdims=True)
    a, b, c, d = (total[i : i + 1] for i in range(4))
    alpha = a / b
    next_rz = a - 2.0 * alpha * b + alpha * alpha * c
    beta = next_rz / a
    bent = b - 2.0 * alpha * c + alpha * alpha * d
    energy = bent + 2.0 * beta * (b - alpha * c) + beta * beta * b
    alpha_next = next_rz / energy
    on_z = jnp.broadcast_to(alpha + alpha_next * (1.0 + beta), (rows, height))
    on_q = jnp.broadcast_to(alpha_next * alpha, (rows, height))

    def finish(i, _):
        for k in range(3):
            x_out[k, i] = on_z * z_s[k, i + HALO, own] - on_q * q_s[k, i + HALO, own]
        return 0

    lax.fori_loop(0, planes, finish, 0, unroll=4)


def per_device(bf, fx, nodes, loads, freq, hw, hb, ow, ob):
    nx, ny = lax.axis_size("gx"), lax.axis_size("gy")
    _, planes, rows, height = bf.shape
    shape = jax.ShapeDtypeStruct
    halo = (2, 3, HALO, rows, height)
    packed = (2, planes, 2, 8, height)
    corner = (2, 2, HALO, 2, 8, height)
    cx, tall, deep = planes // CF + 2, rows + 2 * CF, planes + 2 * HALO
    width = hw.shape[2]
    field = pltpu.VMEM((3, deep, tall, height), f32)
    far = pl.BlockSpec(memory_space=pl.ANY)
    tile = (8, height)
    displacement, density = pl.pallas_call(
        whole_kernel,
        out_shape=[shape(bf.shape, f32), shape(bf.shape[1:], f32)],
        in_specs=[far] * 8 + [pl.BlockSpec(memory_space=pltpu.SMEM)],
        out_specs=[FULL] * 2,
        scratch_shapes=[
            pltpu.VMEM((nodes.shape[1], nodes.shape[0]), jnp.int32),
            pltpu.VMEM(loads.shape, f32),
            pltpu.VMEM(freq.shape, f32),
            pltpu.VMEM(hw.shape, f32),
            pltpu.VMEM(hb.shape, f32),
            pltpu.VMEM((1, width), f32),
            pltpu.VMEM(bf.shape, f32),
            pltpu.VMEM(fx.shape, jnp.int32),
            pltpu.VMEM(halo, f32),
            pltpu.VMEM(halo, jnp.int32),
            pltpu.VMEM(packed, f32),
            pltpu.VMEM(corner, f32),
            pltpu.VMEM(packed, f32),
            pltpu.VMEM((nx - 1, *tile), f32),
            pltpu.VMEM((ny - 1, *tile), f32),
            pltpu.VMEM(tile, f32),
            pltpu.VMEM(tile, f32),
            pltpu.VMEM((hw.shape[0], 2 * width, 2 * width), bf16),
            pltpu.VMEM((cx, tall, height), f32),
            pltpu.VMEM((4, cx, tall, height), f32),
            pltpu.VMEM((deep + 1, tall, height), f32),
            pltpu.VMEM((deep, tall, height), f32),
            field,
            field,
            field,
            field,
            pltpu.VMEM((2, 12, tall, height), f32),
            pltpu.VMEM((12, tall, height), f32),
            pltpu.VMEM((12, tall, height), f32),
            pltpu.VMEM((12, tall, height), f32),
            pltpu.SemaphoreType.DMA((12,)),
            pltpu.SemaphoreType.DMA((10,)),
            pltpu.SemaphoreType.DMA((10,)),
            pltpu.SemaphoreType.DMA((nx + ny - 2,)),
            pltpu.SemaphoreType.DMA((nx + ny - 2,)),
        ],
        compiler_params=pltpu.CompilerParams(
            collective_id=0, has_side_effects=True, vmem_limit_bytes=63 << 20
        ),
    )(bf, fx, nodes.T, loads, freq, hw, hb, ow.reshape(1, -1), ob)
    return jnp.where(fx == 0, displacement, 0.0), density


def solution(mesh):
    grid = P(None, "gx", "gy", None)
    return jax.shard_map(
        per_device,
        mesh=mesh,
        in_specs=(grid, grid, P(), P(), P(), P(), P(), P(), P()),
        out_specs=(grid, P("gx", "gy", None)),
        check_vma=False,
    )
```
